256 devices in a mesh: dp: 4 (over z_hi), ctx: 64 (over y, z_lo, x, core).
Axes of the slice: x: 4, y: 4, z: 8 (z_hi: 4, z_lo: 2; z = z_hi * 2 + z_lo), core: 2. Of those that a mesh axis runs over, the one named last changes fastest.
Arguments:
- resid: bfloat16 [8, 4096, 1536], P('dp', 'ctx'), may hold values from -6 to 6
- queries: bfloat16 [8, 4096, 1536], P('dp', 'ctx'), may hold values from -8 to 8
- keys_in: bfloat16 [8, 4096, 1536], P('dp', 'ctx'), may hold values from -8 to 8
- values: bfloat16 [8, 4096, 1536], P('dp', 'ctx'), may hold values from -6 to 6
- w_out: bfloat16 [1536, 1536], replicated, may hold values from -0.15625 to 0.15625
- slopes: float32 [16], replicated, may hold values from 0.5 to 4
- kernel: float32 [31, 1536], replicated, may hold values from -1 to 1
- lengths: int32 [8], P('dp'), may hold values from 2049 to 4096, as said below
- cotangent: bfloat16 [8, 4096, 1536], P('dp', 'ctx'), may hold values from -6 to 6
Outputs:
- block_out: bfloat16 [8, 4096, 1536], P('dp', 'ctx')
- grad_resid: bfloat16 [8, 4096, 1536], P('dp', 'ctx')
- grad_queries: bfloat16 [8, 4096, 1536], P('dp', 'ctx')
- grad_keys: bfloat16 [8, 4096, 1536], P('dp', 'ctx')
- grad_values: bfloat16 [8, 4096, 1536], P('dp', 'ctx')
- grad_w_out: float32 [1536, 1536], P('ctx')
- grad_kernel: float32 [31, 1536], P(None, 'ctx')
The draws below stay inside these ranges and needn't reach their ends.
Inputs may be any that keep to these rules, and one draw needn't show every extreme that they name: `lengths`: each recording has at least half of its 4096 frames valid, and one recording of the 8 has all of them.
All inputs are finite; a program needn't handle non-finite values.
Results may differ from the reference program's by a relative error of at most 0.02.
Values may be sent and summed in bfloat16 or wider, within the bound.
A program may use at most 128 MiB of HBM per device.

```python
import math
import jax
import jax.numpy as jnp
from jax import lax

HEADS = 16
HEAD_DIM = 96
KW = 31
D = 1536
RECS = 8
FRAMES = 4096


def draw_queries(key, part):
    key = jax.random.fold_in(key, 5)
    base = jnp.clip(jax.random.normal(key, (RECS, FRAMES, HEADS * HEAD_DIM), jnp.float32), -6.0, 6.0)
    return base.astype(jnp.bfloat16)


def draw_keys_in(key, part):
    key = jax.random.fold_in(key, 7)
    base = jnp.clip(jax.random.normal(key, (RECS, FRAMES, HEADS * HEAD_DIM), jnp.float32), -6.0, 6.0)
    return base.astype(jnp.bfloat16)


def draw_lengths(key, part):
    key = jax.random.fold_in(key, 9)
    span_key, pick_key = jax.random.split(key)
    spans = jax.random.randint(span_key, (RECS,), FRAMES // 2 + 1, FRAMES + 1)
    chosen = jax.random.randint(pick_key, (), 0, RECS)
    return jnp.where(jnp.arange(RECS, dtype=jnp.int32) == chosen, FRAMES, spans).astype(jnp.int32)


def steps_of(rng, shape, cuts, smallest, largest):
    gain = 1.0
    for dim, shards_of in cuts:
        heights = jax.random.uniform(jax.random.fold_in(jax.random.fold_in(rng, 6), dim), (shards_of,), jnp.float32, smallest / len(cuts), largest / len(cuts))
        gain = gain * jnp.repeat(jnp.exp(heights), shape[dim] // shards_of).reshape((-1,) + (1,) * (len(shape) - 1 - dim))
    return gain


def noise(stream_key, shape, deviation, bound, cuts=(), held_as=jnp.bfloat16):
    values = deviation * jax.random.normal(stream_key, shape, jnp.float32)
    if cuts:
        values = values * steps_of(stream_key, shape, cuts, -0.22, 0.18)
    return jnp.clip(values, -bound, bound).astype(held_as)


def setup_inputs(seed: int = 0) -> dict:
    seeds = jax.random.split(jax.random.key(seed), 10)
    resid = noise(seeds[0], (RECS, FRAMES, D), 1.0, 6.0, ((0, 4), (1, 64)))
    queries = draw_queries(jax.random.fold_in(seeds[9], 71), 0)
    keys_in = draw_keys_in(jax.random.fold_in(seeds[9], 71), 0)
    values = noise(seeds[3], (RECS, FRAMES, D), 1.0, 6.0, ((0, 4), (1, 64)))
    w_out = noise(seeds[4], (D, D), D ** -0.5, 0.15625)
    slopes = jnp.clip(jnp.exp(jax.random.uniform(seeds[5], (HEADS,), jnp.float32, math.log(0.5), math.log(4.0))), 0.5, 4.0)
    kernel = noise(seeds[6], (KW, D), KW ** -0.5, 1.0, (), jnp.float32)
    lengths = draw_lengths(jax.random.fold_in(seeds[9], 71), 0)
    cotangent = noise(seeds[8], (RECS, FRAMES, D), 1.0, 6.0, ((0, 4), (1, 64)))
    return dict(resid=resid, queries=queries, keys_in=keys_in, values=values, w_out=w_out, slopes=slopes, kernel=kernel, lengths=lengths, cotangent=cotangent)


def head_pairs(array):
    return array.reshape(RECS, FRAMES, HEADS, HEAD_DIM).transpose(0, 2, 1, 3).reshape(RECS * HEADS, FRAMES, HEAD_DIM)

def frame_rows(array):
    return array.reshape(RECS, HEADS, FRAMES, HEAD_DIM).transpose(0, 2, 1, 3).reshape(RECS, FRAMES, HEADS * HEAD_DIM)

def probability(query_block, key_block, slope_rate, length):
    inverse = 1.0 / math.sqrt(HEAD_DIM)
    places = jnp.arange(FRAMES, dtype=jnp.int32)
    distance = jnp.abs(places[:, None] - places[None, :]).astype(jnp.float32)
    scores = jnp.dot(query_block, key_block.T, preferred_element_type=jnp.float32) * inverse - slope_rate / FRAMES * distance
    scores = jnp.where((places < length)[None, :], scores, -1e+30)
    row_max = lax.optimization_barrier(jnp.max(scores, axis=1, keepdims=True))
    exponent = jnp.exp(scores - row_max)
    return exponent / lax.optimization_barrier(jnp.sum(exponent, axis=1, keepdims=True))

def forward_pair(members):
    query_block, key_block, value_block, slope_rate, length = members
    probs = probability(query_block, key_block, slope_rate, length)
    return jnp.dot(probs.astype(jnp.bfloat16), value_block, preferred_element_type=jnp.float32).astype(jnp.bfloat16)

def backward_pair(members):
    query_block, key_block, value_block, grad_block, slope_rate, length = members
    inverse = 1.0 / math.sqrt(HEAD_DIM)
    probs = probability(query_block, key_block, slope_rate, length)
    weights = probs.astype(jnp.bfloat16)
    dprob = jnp.dot(grad_block, value_block.T, preferred_element_type=jnp.float32)
    row_dot = lax.optimization_barrier(jnp.sum(probs * dprob, axis=1, keepdims=True))
    dscore = (probs * (dprob - row_dot)).astype(jnp.bfloat16)
    grad_query = (jnp.dot(dscore, key_block, preferred_element_type=jnp.float32) * inverse).astype(jnp.bfloat16)
    grad_key = (jnp.dot(dscore.T, query_block, preferred_element_type=jnp.float32) * inverse).astype(jnp.bfloat16)
    grad_value = jnp.dot(weights.T, grad_block, preferred_element_type=jnp.float32).astype(jnp.bfloat16)
    return (grad_query, grad_key, grad_value)

def reference(resid, queries, keys_in, values, w_out, slopes, kernel, lengths, cotangent):
    slope_pairs = jnp.tile(slopes, RECS)
    length_pairs = jnp.repeat(lengths, HEADS)
    query_pairs = head_pairs(queries)
    key_pairs = head_pairs(keys_in)
    value_pairs = head_pairs(values)
    attended_pairs = lax.map(forward_pair, (query_pairs, key_pairs, value_pairs, slope_pairs, length_pairs))
    attended = frame_rows(attended_pairs)
    mixed = jnp.dot(attended.reshape(RECS * FRAMES, D), w_out, preferred_element_type=jnp.float32).reshape(RECS, FRAMES, D)
    stream = (resid.astype(jnp.float32) + mixed).astype(jnp.bfloat16)
    live_mask = (jnp.arange(FRAMES, dtype=jnp.int32)[None, :] < lengths[:, None])[:, :, None]
    masked = jnp.where(live_mask, stream, jnp.zeros_like(stream))
    half_span = KW // 2
    padded = jnp.pad(masked, ((0, 0), (half_span, half_span), (0, 0)))
    convolved = jnp.zeros((RECS, FRAMES, D), jnp.float32)
    for offset in range(KW):
        convolved = convolved + kernel[offset] * padded[:, offset:offset + FRAMES].astype(jnp.float32)
    block_out = (stream.astype(jnp.float32) + jax.nn.silu(convolved)).astype(jnp.bfloat16)
    squash = jax.nn.sigmoid(convolved)
    conv_grad = (cotangent.astype(jnp.float32) * squash * (1.0 + convolved * (1.0 - squash))).astype(jnp.bfloat16)
    grad_padded = jnp.pad(conv_grad, ((0, 0), (half_span, half_span), (0, 0)))
    back_conv = jnp.zeros((RECS, FRAMES, D), jnp.float32)
    for offset in range(KW):
        first_row = 2 * half_span - offset
        back_conv = back_conv + kernel[offset] * grad_padded[:, first_row:first_row + FRAMES].astype(jnp.float32)
    grad_stream = cotangent.astype(jnp.float32) + jnp.where(live_mask, back_conv, jnp.zeros_like(back_conv))
    grad_resid = grad_stream.astype(jnp.bfloat16)
    grad_scale = 1.0 / math.sqrt(RECS * FRAMES)
    grad_w_out = jnp.dot(attended.reshape(RECS * FRAMES, D).T, grad_resid.reshape(RECS * FRAMES, D), preferred_element_type=jnp.float32) * grad_scale
    kernel_terms = []
    for offset in range(KW):
        kernel_terms.append(lax.optimization_barrier(jnp.sum(conv_grad.astype(jnp.float32) * padded[:, offset:offset + FRAMES].astype(jnp.float32), axis=(0, 1))))
    grad_kernel = jnp.stack(kernel_terms) * grad_scale
    grad_attended = lax.dot_general(grad_resid.reshape(RECS * FRAMES, D), w_out, (((1,), (1,)), ((), ())), preferred_element_type=jnp.float32).astype(jnp.bfloat16).reshape(RECS, FRAMES, D)
    grad_query, grad_key, grad_value = lax.map(backward_pair, (query_pairs, key_pairs, value_pairs, head_pairs(grad_attended), slope_pairs, length_pairs))
    return (block_out, grad_resid, frame_rows(grad_query), frame_rows(grad_key), frame_rows(grad_value), grad_w_out, grad_kernel)
```

```python
import math

import jax
import jax.numpy as jnp
from jax import lax
from jax.experimental import pallas as pl
from jax.experimental.pallas import tpu as pltpu
from jax.sharding import PartitionSpec as P

HEADS = 16
HEAD_DIM = 96


def padded_2(x, sides, width):
    for axis, dim in sides:
        size, length = (lax.axis_size(axis), x.shape[dim])
        up = [(i, (i + 1) % size) for i in range(size - 1)]
        down = [(j, i) for i, j in up]
        last = lax.slice_in_dim(x, length - width, length, axis=dim)
        first = lax.slice_in_dim(x, 0, width, axis=dim)
        before = lax.ppermute(last, axis, up)
        after = lax.ppermute(first, axis, down)
        x = jnp.concatenate([before, x, after], axis=dim)
    return x


def to_pairs(array, head_count, head_width):
    record_count, frames_here, model_width = array.shape
    return (
        array.reshape(record_count, frames_here, head_count, head_width)
        .transpose(0, 2, 1, 3)
        .reshape(record_count * head_count, frames_here * head_width)
    )


def spread_pairs(array, head_count, head_width, copies):
    pairs = to_pairs(array, head_count, head_width)
    pairs = jnp.repeat(pairs, copies, axis=0)
    return pairs


def to_frames(array, record_count, head_count, head_width):
    frames_here = array.shape[1] // head_width
    return (
        array.reshape(record_count, head_count, frames_here, head_width)
        .transpose(0, 2, 1, 3)
        .reshape(record_count, frames_here, head_count * head_width)
    )


def share_slots(block, copies, part):
    pair_count, width = block.shape
    pieces = block.reshape(pair_count, 1, width)
    slots = (jnp.arange(copies, dtype=jnp.int32) == part)[None, :, None]
    placed = jnp.where(slots, pieces, jnp.zeros_like(pieces))
    return placed.reshape(pair_count, copies * width)


def collect_shares(received, copies, pair_count):
    width = received.shape[1]
    grouped = received.reshape(-1, copies, pair_count, width)
    return jnp.sum(grouped, axis=1).reshape(-1, width)


def pick_small(lookup, position, entries):
    matches = position[:, None] == jnp.arange(entries, dtype=jnp.int32)[None, :]
    return jnp.sum(jnp.where(matches, lookup[None, :], jnp.zeros_like(lookup)[None, :]), axis=1)


def block_scores(query_rows, key_block, slope_rate, length, query_place, frames, inverse):
    key_place = jnp.arange(frames, dtype=jnp.int32)
    distance = jnp.abs(query_place[:, None] - key_place[None, :]).astype(jnp.float32)
    scores = (
        jnp.dot(query_rows, key_block.T, preferred_element_type=jnp.float32) * inverse
        - slope_rate / frames * distance
    )
    return jnp.where((key_place < length)[None, :], scores, -1e30)


def attend(query_share, key_block, value_block, slope_rate, length, query_place, block_rows):
    share_rows, head_width = query_share.shape
    frames = key_block.shape[0]
    inverse = 1.0 / math.sqrt(head_width)

    def per_block(step):
        first_row = step * block_rows
        query_rows = lax.dynamic_slice_in_dim(query_share, first_row, block_rows, 0)
        place_rows = lax.dynamic_slice_in_dim(query_place, first_row, block_rows, 0)
        scores = block_scores(
            query_rows, key_block, slope_rate, length, place_rows, frames, inverse
        )
        row_max = jnp.max(scores, axis=1, keepdims=True)
        exponent = jnp.exp(scores - row_max)
        row_sum = jnp.sum(exponent, axis=1, keepdims=True)
        probs = exponent / row_sum
        result = jnp.dot(
            probs.astype(jnp.bfloat16), value_block, preferred_element_type=jnp.float32
        ).astype(jnp.bfloat16)
        return (result, (row_max + jnp.log(row_sum))[:, 0])

    results, log_total = lax.map(per_block, jnp.arange(share_rows // block_rows, dtype=jnp.int32))
    return (results.reshape(share_rows, head_width), log_total.reshape(share_rows))


def attend_back(
    query_share,
    key_block,
    value_block,
    grad_share,
    log_total,
    slope_rate,
    length,
    query_place,
    block_rows,
):
    share_rows, head_width = query_share.shape
    frames = key_block.shape[0]
    inverse = 1.0 / math.sqrt(head_width)

    def per_block(carried, step):
        key_acc, value_acc = carried
        first_row = step * block_rows
        query_rows = lax.dynamic_slice_in_dim(query_share, first_row, block_rows, 0)
        grad_rows = lax.dynamic_slice_in_dim(grad_share, first_row, block_rows, 0)
        total_rows = lax.dynamic_slice_in_dim(log_total, first_row, block_rows, 0)
        place_rows = lax.dynamic_slice_in_dim(query_place, first_row, block_rows, 0)
        scores = block_scores(
            query_rows, key_block, slope_rate, length, place_rows, frames, inverse
        )
        probs = jnp.exp(scores - total_rows[:, None])
        weights = probs.astype(jnp.bfloat16)
        dprob = jnp.dot(grad_rows, value_block.T, preferred_element_type=jnp.float32)
        row_dot = jnp.sum(probs * dprob, axis=1, keepdims=True)
        dscore = (probs * (dprob - row_dot)).astype(jnp.bfloat16)
        grad_query = jnp.dot(dscore, key_block, preferred_element_type=jnp.float32) * inverse
        key_acc = key_acc + jnp.dot(dscore.T, query_rows, preferred_element_type=jnp.float32)
        value_acc = value_acc + jnp.dot(weights.T, grad_rows, preferred_element_type=jnp.float32)
        return ((key_acc, value_acc), grad_query)

    empty = jnp.zeros((frames, head_width), jnp.float32)
    sums, grad_query = lax.scan(
        per_block, (empty, empty), jnp.arange(share_rows // block_rows, dtype=jnp.int32)
    )
    return (grad_query.reshape(share_rows, head_width), sums[0] * inverse, sums[1])


MESH = pl.DeviceIdType.MESH
TILE = 128


def barrier_all(me, count):
    barrier = pltpu.get_barrier_semaphore()

    def greet(step, carry):
        other = lax.rem(me + step, count)
        pl.semaphore_signal(barrier, inc=1, device_id={"ctx": other}, device_id_type=MESH)
        return carry

    lax.fori_loop(1, count, greet, 0)
    pl.semaphore_wait(barrier, count - 1)


def arrived(ref, sem):
    pltpu.make_async_copy(ref, ref, sem).wait()


def spread_kernel(
    q_ref, k_ref, v_ref, resid_ref, cot_ref,
    qt_ref, kvt_ref, resid_out, cot_out,
    halves, send_q, send_kv,
    swap_send, swap_recv, swap_local, q_send, kv_send, q_recv, kv_recv, fwd_send,
):
    me = lax.axis_index("ctx")
    core = lax.rem(me, 2)
    chip = me // 2
    sibling = me + 1 - 2 * core
    barrier_all(me, 64)

    rows = pl.ds(pl.multiple_of(core * 64, 64), 64)
    sources = [q_ref, k_ref, v_ref, resid_ref, cot_ref]
    targets = [halves.at[0], halves.at[1], halves.at[2], resid_out, cot_out]
    swaps = []
    for n in range(5):
        there = pltpu.make_async_remote_copy(
            src_ref=sources[n].at[1 - core],
            dst_ref=targets[n].at[rows],
            send_sem=swap_send.at[n],
            recv_sem=swap_recv.at[n],
            device_id={"ctx": sibling},
            device_id_type=MESH,
        )
        here = pltpu.make_async_copy(sources[n].at[core], targets[n].at[rows], swap_local.at[n])
        there.start()
        here.start()
        swaps.append((there, here))

    def turn(n):
        there, here = swaps[n]
        here.wait()
        there.wait_recv()
        for t in range(12):
            flipped = halves[n, :, t * TILE : (t + 1) * TILE].T
            for u in range(4):
                feature = t * TILE + u * 32
                head, place = feature // 96, feature % 96
                piece = flipped[u * 32 : (u + 1) * 32]
                if n == 0:
                    send_q[head, place : place + 32, :] = piece
                else:
                    first = place + (n - 1) * 96
                    send_kv[head, first : first + 32, :] = piece

    half = chip // 16
    parity = lax.rem(chip, 2)

    def send(buffer, target, slot, target_core, send_sems, recv_sem):
        def one(step, carry):
            head = lax.rem(step + chip, 16)
            other = (core * 16 + head) * 2 + target_core

            @pl.when(other != me)
            def _():
                pltpu.make_async_remote_copy(
                    src_ref=buffer.at[head],
                    dst_ref=target.at[slot],
                    send_sem=send_sems.at[head],
                    recv_sem=recv_sem,
                    device_id={"ctx": other},
                    device_id_type=MESH,
                ).start()

            @pl.when(other == me)
            def _():
                pltpu.make_async_copy(buffer.at[head], target.at[slot], recv_sem).start()

            return carry

        lax.fori_loop(0, 16, one, 0)

    def sent(buffer, target_core, send_sems):
        def one(head, carry):
            other = (core * 16 + head) * 2 + target_core

            @pl.when(other != me)
            def _():
                arrived(buffer.at[head], send_sems.at[head])

            return carry

        lax.fori_loop(0, 16, one, 0)

    turn(1)
    turn(2)
    send(send_kv, kvt_ref, chip, parity, kv_send, kv_recv.at[chip])
    turn(0)
    send(send_q, qt_ref, lax.rem(chip, 16), half, q_send, q_recv.at[lax.rem(chip, 16)])

    def forward(step, carry):
        slot = 2 * lax.rem(step + chip // 2, 16) + core
        arrived(kvt_ref.at[slot], kv_recv.at[slot])
        pltpu.make_async_remote_copy(
            src_ref=kvt_ref.at[slot],
            dst_ref=kvt_ref.at[slot],
            send_sem=fwd_send.at[slot // 2],
            recv_sem=kv_recv.at[slot],
            device_id={"ctx": sibling},
            device_id_type=MESH,
        ).start()
        return carry

    lax.fori_loop(0, 16, forward, 0)

    def finish(step, carry):
        arrived(qt_ref.at[step], q_recv.at[step])
        other = 2 * step + 1 - core
        arrived(kvt_ref.at[other], kv_recv.at[other])
        mine = 2 * step + core
        arrived(kvt_ref.at[mine], fwd_send.at[step])
        return carry

    lax.fori_loop(0, 16, finish, 0)
    sent(send_kv, parity, kv_send)
    sent(send_q, half, q_send)
    for n in range(5):
        there, here = swaps[n]
        there.wait_send()
        if n >= 3:
            here.wait()
            there.wait_recv()


def spread_heads(queries, keys_in, values, resid, cotangent):
    bf16 = jnp.bfloat16
    any_space = pl.BlockSpec(memory_space=pl.ANY)
    return pl.pallas_call(
        spread_kernel,
        out_shape=(
            jax.ShapeDtypeStruct((16, 96, 128), bf16),
            jax.ShapeDtypeStruct((32, 192, 128), bf16),
            jax.ShapeDtypeStruct((128, 1536), bf16),
            jax.ShapeDtypeStruct((128, 1536), bf16),
        ),
        in_specs=[any_space] * 5,
        out_specs=[any_space] * 4,
        scratch_shapes=[
            pltpu.VMEM((3, 128, 1536), bf16),
            pltpu.VMEM((16, 96, 128), bf16),
            pltpu.VMEM((16, 192, 128), bf16),
            pltpu.SemaphoreType.DMA((5,)),
            pltpu.SemaphoreType.DMA((5,)),
            pltpu.SemaphoreType.DMA((5,)),
            pltpu.SemaphoreType.DMA((16,)),
            pltpu.SemaphoreType.DMA((16,)),
            pltpu.SemaphoreType.DMA((16,)),
            pltpu.SemaphoreType.DMA((32,)),
            pltpu.SemaphoreType.DMA((16,)),
        ],
        compiler_params=pltpu.CompilerParams(collective_id=0, has_side_effects=True),
        name="spread_heads",
    )(queries, keys_in, values, resid, cotangent)


def per_device(resid, queries, keys_in, values, w_out, slopes, kernel, lengths, cotangent):
    record_count, frames_here, model_width = resid.shape
    ctx_count = lax.axis_size("ctx")
    position = lax.axis_index("ctx")
    head_count = HEADS
    head_width = HEAD_DIM
    frames = frames_here * ctx_count
    pair_total = record_count * head_count
    pair_count = max(1, pair_total // ctx_count)
    copies = max(1, ctx_count // pair_total)
    share_rows = frames // copies
    part = position % copies
    block_rows = 512
    row_count = record_count * frames_here
    pair_ids = (position * pair_count + jnp.arange(pair_count, dtype=jnp.int32)) // copies
    pair_slopes = pick_small(slopes, pair_ids % head_count, head_count)
    pair_lengths = pick_small(lengths, pair_ids // head_count, record_count)
    query_start = part * share_rows
    query_place = query_start + jnp.arange(share_rows, dtype=jnp.int32)
    query_tiles, pair_tiles, _, _ = spread_heads(queries, keys_in, values, resid, cotangent)
    query_heads = query_tiles.transpose(0, 2, 1).reshape(1, share_rows, head_width)
    key_heads = pair_tiles[:, :head_width].transpose(0, 2, 1).reshape(1, frames, head_width)
    value_heads = pair_tiles[:, head_width:].transpose(0, 2, 1).reshape(1, frames, head_width)

    def forward_one(members):
        return attend(
            members[0], members[1], members[2], members[3], members[4], query_place, block_rows
        )

    result_heads, log_total = lax.map(
        forward_one, (query_heads, key_heads, value_heads, pair_slopes, pair_lengths)
    )
    outgoing = share_slots(result_heads.reshape(pair_count, share_rows * head_width), copies, part)
    returned = lax.all_to_all(outgoing, "ctx", split_axis=1, concat_axis=0, tiled=True)
    attended_pairs = collect_shares(returned, copies, pair_count)
    attended = to_frames(attended_pairs, record_count, head_count, head_width)
    mixed = jnp.dot(
        attended.reshape(row_count, model_width), w_out, preferred_element_type=jnp.float32
    ).reshape(record_count, frames_here, model_width)
    stream = (resid.astype(jnp.float32) + mixed).astype(jnp.bfloat16)
    frame_place = position * frames_here + jnp.arange(frames_here, dtype=jnp.int32)
    live_mask = (frame_place[None, :] < lengths[:, None])[:, :, None]
    masked = jnp.where(live_mask, stream, jnp.zeros_like(stream))
    taps = kernel.shape[0]
    half_span = taps // 2
    padded = padded_2(masked, (("ctx", 1),), half_span)
    convolved = jnp.zeros((record_count, frames_here, model_width), jnp.float32)
    for offset in range(taps):
        convolved = convolved + kernel[offset] * padded[:, offset : offset + frames_here].astype(
            jnp.float32
        )
    block_out = (stream.astype(jnp.float32) + jax.nn.silu(convolved)).astype(jnp.bfloat16)
    squash = jax.nn.sigmoid(convolved)
    conv_grad = (
        cotangent.astype(jnp.float32) * squash * (1.0 + convolved * (1.0 - squash))
    ).astype(jnp.bfloat16)
    grad_padded = padded_2(conv_grad, (("ctx", 1),), half_span)
    back_conv = jnp.zeros((record_count, frames_here, model_width), jnp.float32)
    for offset in range(taps):
        first_row = 2 * half_span - offset
        back_conv = back_conv + kernel[offset] * grad_padded[
            :, first_row : first_row + frames_here
        ].astype(jnp.float32)
    grad_stream = cotangent.astype(jnp.float32) + jnp.where(
        live_mask, back_conv, jnp.zeros_like(back_conv)
    )
    grad_resid = grad_stream.astype(jnp.bfloat16)
    grad_flat = grad_resid.reshape(row_count, model_width)
    weight_term = lax.dot_general(
        attended.reshape(row_count, model_width),
        grad_flat,
        (((0,), (0,)), ((), ())),
        preferred_element_type=jnp.float32,
    )
    kernel_list = []
    for offset in range(taps):
        kernel_list.append(
            jnp.sum(
                conv_grad.astype(jnp.float32)
                * padded[:, offset : offset + frames_here].astype(jnp.float32),
                axis=(0, 1),
            )
        )
    kernel_term = jnp.stack(kernel_list)
    grad_attended = lax.dot_general(
        grad_flat, w_out, (((1,), (1,)), ((), ())), preferred_element_type=jnp.float32
    ).astype(jnp.bfloat16)
    grad_attended = grad_attended.reshape(record_count, frames_here, model_width)
    grad_heads = lax.all_to_all(
        spread_pairs(grad_attended, head_count, head_width, copies),
        "ctx",
        split_axis=0,
        concat_axis=1,
        tiled=True,
    )
    grad_heads = lax.dynamic_slice_in_dim(
        grad_heads.reshape(pair_count, frames, head_width), part * share_rows, share_rows, 1
    )

    def backward_one(members):
        return attend_back(
            members[0],
            members[1],
            members[2],
            members[3],
            members[4],
            members[5],
            members[6],
            query_place,
            block_rows,
        )

    grad_query, grad_key, grad_value = lax.map(
        backward_one,
        (query_heads, key_heads, value_heads, grad_heads, log_total, pair_slopes, pair_lengths),
    )
    query_out = share_slots(grad_query.reshape(pair_count, share_rows * head_width), copies, part)
    query_back, key_back, value_back = (
        lax.all_to_all(
            query_out.astype(jnp.bfloat16), "ctx", split_axis=1, concat_axis=0, tiled=True
        ).astype(query_out.dtype),
        lax.all_to_all(
            grad_key.reshape(pair_count, frames * head_width).astype(jnp.bfloat16),
            "ctx",
            split_axis=1,
            concat_axis=0,
            tiled=True,
        ).astype(jnp.float32),
        lax.all_to_all(
            grad_value.reshape(pair_count, frames * head_width).astype(jnp.bfloat16),
            "ctx",
            split_axis=1,
            concat_axis=0,
            tiled=True,
        ).astype(jnp.float32),
    )
    query_back = collect_shares(query_back, copies, pair_count).astype(jnp.bfloat16)
    key_back = collect_shares(key_back, copies, pair_count).astype(jnp.bfloat16)
    value_back = collect_shares(value_back, copies, pair_count).astype(jnp.bfloat16)
    grad_scale = 1.0 / math.sqrt(lax.axis_size("dp") * record_count * frames)
    weight_pieces = lax.all_to_all(
        weight_term.astype(jnp.bfloat16), "ctx", split_axis=0, concat_axis=0, tiled=True
    )
    weight_part = jnp.sum(
        weight_pieces.reshape(ctx_count, -1, model_width).astype(jnp.float32), axis=0
    )
    kernel_part = lax.psum_scatter(kernel_term, "ctx", scatter_dimension=1, tiled=True)
    weight_sum, kernel_sum = (
        lax.psum(weight_part.astype(jnp.bfloat16), "dp").astype(jnp.float32),
        lax.psum(kernel_part.astype(jnp.bfloat16), "dp").astype(jnp.float32),
    )
    grad_w_out = weight_sum * grad_scale
    grad_kernel = kernel_sum * grad_scale
    return (
        block_out,
        grad_resid,
        to_frames(query_back, record_count, head_count, head_width),
        to_frames(key_back, record_count, head_count, head_width),
        to_frames(value_back, record_count, head_count, head_width),
        grad_w_out,
        grad_kernel,
    )


def solution(mesh):
    in_specs = (
        P("dp", "ctx", None),
        P("dp", "ctx", None),
        P("dp", "ctx", None),
        P("dp", "ctx", None),
        P(),
        P(),
        P(),
        P("dp"),
        P("dp", "ctx", None),
    )
    out_specs = (
        P("dp", "ctx", None),
        P("dp", "ctx", None),
        P("dp", "ctx", None),
        P("dp", "ctx", None),
        P("dp", "ctx", None),
        P("ctx", None),
        P(None, "ctx"),
    )
    return jax.shard_map(
        per_device, mesh=mesh, in_specs=in_specs, out_specs=out_specs, check_vma=False
    )
```

```python
import math

import jax
import jax.numpy as jnp
from jax import lax
from jax.experimental import pallas as pl
from jax.experimental.pallas import tpu as pltpu
from jax.sharding import PartitionSpec as P

F32 = jnp.float32
BF16 = jnp.bfloat16
VMEM_BYTES = 56 * 1024 * 1024
ANY = pl.BlockSpec(memory_space=pl.ANY)
IN_VMEM = pl.BlockSpec(memory_space=pltpu.VMEM)
IN_SMEM = pl.BlockSpec(memory_space=pltpu.SMEM)
FRAMES = 4096
SCALE = 1.0 / math.sqrt(96)
LOG2E = math.log2(math.e)
MESH = pl.DeviceIdType.MESH
TILE = 128


def barrier_all(me, count, groups=1):
    barrier = pltpu.get_barrier_semaphore()
    here = lax.axis_index("dp")

    def greet(step, carry):
        other = lax.rem(me + step, count)
        pl.semaphore_signal(barrier, inc=1, device_id={"ctx": other}, device_id_type=MESH)
        return carry

    lax.fori_loop(1, count, greet, 0)
    for step in range(1, groups):
        other = lax.rem(here + step, groups)
        pl.semaphore_signal(barrier, inc=1, device_id={"dp": other}, device_id_type=MESH)
    pl.semaphore_wait(barrier, count + groups - 2)


def arrived(ref, sem):
    pltpu.make_async_copy(ref, ref, sem).wait()


def send_heads(me, buffer, target, slot, target_core, send_sems, recv_sem):
    core, chip = lax.rem(me, 2), me // 2

    def one(step, carry):
        head = lax.rem(step + chip, 16)
        send_block(
            me,
            (core * 16 + head) * 2 + target_core,
            buffer.at[head],
            target.at[slot],
            send_sems.at[head],
            recv_sem,
        )
        return carry

    lax.fori_loop(0, 16, one, 0)


def send_block(me, other, source, target, send_sem, recv_sem):
    @pl.when(other != me)
    def _():
        pltpu.make_async_remote_copy(
            src_ref=source,
            dst_ref=target,
            send_sem=send_sem,
            recv_sem=recv_sem,
            device_id={"ctx": other},
            device_id_type=MESH,
        ).start()

    @pl.when(other == me)
    def _():
        pltpu.make_async_copy(source, target, recv_sem).start()


def heads_sent(me, buffer, target_core, send_sems):
    core = lax.rem(me, 2)

    def one(head, carry):
        other = (core * 16 + head) * 2 + target_core

        @pl.when(other != me)
        def _():
            arrived(buffer.at[head], send_sems.at[head])

        return carry

    lax.fori_loop(0, 16, one, 0)


def remote(source, target, send_sem, recv_sem, **device):
    return pltpu.make_async_remote_copy(
        src_ref=source,
        dst_ref=target,
        send_sem=send_sem,
        recv_sem=recv_sem,
        device_id=device,
        device_id_type=MESH,
    )


def spread_kernel(
    q_ref, k_ref, v_ref, resid_ref, cot_ref,
    qt_ref, kvt_ref, resid_out, cot_out,
    halves, send_q, send_kv,
    swap_send, swap_recv, swap_local, q_send, kv_send, q_recv, kv_recv, fwd_send,
):
    me = lax.axis_index("ctx")
    core = lax.rem(me, 2)
    chip = me // 2
    sibling = me + 1 - 2 * core
    barrier_all(me, 64)

    rows = pl.ds(pl.multiple_of(core * 64, 64), 64)
    sources = [q_ref, k_ref, v_ref, resid_ref, cot_ref]
    targets = [halves.at[0], halves.at[1], halves.at[2], resid_out, cot_out]
    swaps = []
    for n in range(5):
        there = pltpu.make_async_remote_copy(
            src_ref=sources[n].at[1 - core],
            dst_ref=targets[n].at[rows],
            send_sem=swap_send.at[n],
            recv_sem=swap_recv.at[n],
            device_id={"ctx": sibling},
            device_id_type=MESH,
        )
        here = pltpu.make_async_copy(sources[n].at[core], targets[n].at[rows], swap_local.at[n])
        there.start()
        here.start()
        swaps.append((there, here))

    def turn(n):
        there, here = swaps[n]
        here.wait()
        there.wait_recv()
        for t in range(12):
            flipped = halves[n, :, t * TILE : (t + 1) * TILE].T
            for u in range(4):
                feature = t * TILE + u * 32
                head, place = feature // 96, feature % 96
                piece = flipped[u * 32 : (u + 1) * 32]
                if n == 0:
                    send_q[head, place : place + 32, :] = piece
                else:
                    first = place + (n - 1) * 96
                    send_kv[head, first : first + 32, :] = piece

    half = chip // 16
    parity = lax.rem(chip, 2)

    turn(1)
    turn(2)
    send_heads(me, send_kv, kvt_ref, chip, parity, kv_send, kv_recv.at[chip])
    turn(0)
    place = lax.rem(chip, 16)
    send_heads(me, send_q, qt_ref, place, half, q_send, q_recv.at[place])

    def forward(step, carry):
        slot = 2 * lax.rem(step + chip // 2, 16) + core
        arrived(kvt_ref.at[slot], kv_recv.at[slot])
        pltpu.make_async_remote_copy(
            src_ref=kvt_ref.at[slot],
            dst_ref=kvt_ref.at[slot],
            send_sem=fwd_send.at[slot // 2],
            recv_sem=kv_recv.at[slot],
            device_id={"ctx": sibling},
            device_id_type=MESH,
        ).start()
        return carry

    lax.fori_loop(0, 16, forward, 0)

    def finish(step, carry):
        arrived(qt_ref.at[step], q_recv.at[step])
        other = 2 * step + 1 - core
        arrived(kvt_ref.at[other], kv_recv.at[other])
        mine = 2 * step + core
        arrived(kvt_ref.at[mine], fwd_send.at[step])
        return carry

    lax.fori_loop(0, 16, finish, 0)
    heads_sent(me, send_kv, parity, kv_send)
    heads_sent(me, send_q, half, q_send)
    for n in range(5):
        there, here = swaps[n]
        there.wait_send()
        if n >= 3:
            here.wait()
            there.wait_recv()


def spread_heads(queries, keys_in, values, resid, cotangent):
    bf16 = jnp.bfloat16
    any_space = pl.BlockSpec(memory_space=pl.ANY)
    return pl.pallas_call(
        spread_kernel,
        out_shape=(
            jax.ShapeDtypeStruct((16, 96, 128), bf16),
            jax.ShapeDtypeStruct((32, 192, 128), bf16),
            jax.ShapeDtypeStruct((128, 1536), bf16),
            jax.ShapeDtypeStruct((128, 1536), bf16),
        ),
        in_specs=[any_space] * 5,
        out_specs=[any_space] * 4,
        scratch_shapes=[
            pltpu.VMEM((3, 128, 1536), bf16),
            pltpu.VMEM((16, 96, 128), bf16),
            pltpu.VMEM((16, 192, 128), bf16),
            pltpu.SemaphoreType.DMA((5,)),
            pltpu.SemaphoreType.DMA((5,)),
            pltpu.SemaphoreType.DMA((5,)),
            pltpu.SemaphoreType.DMA((16,)),
            pltpu.SemaphoreType.DMA((16,)),
            pltpu.SemaphoreType.DMA((16,)),
            pltpu.SemaphoreType.DMA((32,)),
            pltpu.SemaphoreType.DMA((16,)),
        ],
        compiler_params=pltpu.CompilerParams(collective_id=0, has_side_effects=True),
        name="spread_heads",
    )(queries, keys_in, values, resid, cotangent)


def three_parts(value):
    first = value.astype(BF16).astype(F32)
    second = (value - first).astype(BF16).astype(F32)
    return first, second, value - first - second


def key_rows(tile, length):
    row = lax.broadcasted_iota(jnp.int32, (64, TILE), 0)
    frame = tile * TILE + lax.broadcasted_iota(jnp.int32, (64, TILE), 1)
    low = lax.rem(frame, 64)
    hidden = jnp.where(frame < length, 0.0, -1e30)
    place = jnp.where(lax.rem(row, 2) == 0, frame - low, low).astype(F32)
    return jnp.where(
        row < 6, place, jnp.where(row < 9, 1.0, jnp.where(row == 9, hidden, 0.0))
    ).astype(BF16)


def query_rows(first_frame, rate):
    row = lax.broadcasted_iota(jnp.int32, (64, TILE), 0)
    frame = first_frame + lax.broadcasted_iota(jnp.int32, (64, TILE), 1)
    rates = three_parts(jnp.full((64, TILE), rate, F32))
    shifts = three_parts(rate * frame.astype(F32))
    rows = jnp.zeros((64, TILE), F32)
    for n in range(3):
        rows = jnp.where(row // 2 == n, rates[n], rows)
        rows = jnp.where(row == 6 + n, -shifts[n], rows)
    one = jnp.where(row == 9, 1.0, 0.0)
    return (rows + one).astype(BF16), (one - rows).astype(BF16)


def forward_kernel(
    slopes_ref, lengths_ref, qt_ref, kvt_ref,
    att_ref, mean_ref, probs_ref,
    keys, value_rows, query_cols, scores, weights, tops, out_sems,
):
    me = lax.axis_index("ctx")
    core, chip = lax.rem(me, 2), me // 2
    rate = slopes_ref[lax.rem(chip, 16)] * (LOG2E / FRAMES)
    length = lengths_ref[chip // 16]

    def build_keys(tile, carry):
        kt = kvt_ref[tile, 0:96, :]
        wide = jnp.concatenate([kt, kt, key_rows(tile, length)], axis=0)
        keys[pl.ds(pl.multiple_of(tile * TILE, TILE), TILE), :] = wide.T
        lanes = pl.ds(pl.multiple_of(lax.rem(tile, 4) * TILE, TILE), TILE)
        one = lax.broadcasted_iota(jnp.int32, (32, TILE), 0) == 0
        value_rows[tile // 4, 0:96, lanes] = kvt_ref[tile, 96:192, :]
        value_rows[tile // 4, 96:128, lanes] = jnp.where(one, 1.0, 0.0).astype(BF16)
        return carry

    lax.fori_loop(0, 32, build_keys, 0)

    def build_queries(tile, carry):
        scaled = qt_ref[tile].astype(F32) * (SCALE * LOG2E)
        high = scaled.astype(BF16)
        low = (scaled - high.astype(F32)).astype(BF16)
        before, after = query_rows(core * 2048 + tile * TILE, rate)
        lanes = pl.ds(pl.multiple_of(lax.rem(tile, 2) * TILE, TILE), TILE)
        query_cols[tile // 2, 0, :, lanes] = jnp.concatenate([high, low, before], axis=0)
        query_cols[tile // 2, 1, :, lanes] = jnp.concatenate([high, low, after], axis=0)
        return carry

    lax.fori_loop(0, 16, build_queries, 0)

    def diagonal(block):
        return core * 4 + block // 2

    def chunk_of(block, step):
        return lax.rem(diagonal(block) + 1 + step, 8)

    def chunk_rows(chunk):
        return pl.ds(pl.multiple_of(chunk * 512, 512), 512)

    def score(block, slot, step, top):
        chunk = chunk_of(block, step)
        side = jnp.where(chunk > diagonal(block), 1, 0)
        result = jnp.dot(
            keys[chunk_rows(chunk), :], query_cols[block, side], preferred_element_type=F32
        )
        scores[slot, chunk_rows(chunk), :] = result
        return jnp.maximum(top, jnp.max(result.reshape(64, 8, 256), axis=0))

    def weigh(block, slot, step, top, total, last):
        chunk = chunk_of(block, step)
        shifted = scores[slot, chunk_rows(chunk), :] - top
        if last:
            key = chunk * 512 + lax.broadcasted_iota(jnp.int32, (512, 256), 0)
            query = core * 2048 + block * 256 + lax.broadcasted_iota(jnp.int32, (512, 256), 1)
            ahead = jnp.maximum(key - query, 0).astype(F32)
            shifted = shifted - (2.0 * rate) * ahead
        weight = jnp.exp2(shifted).astype(BF16)
        weights[slot, chunk] = weight
        return total + jnp.dot(value_rows[chunk], weight, preferred_element_type=F32)

    lowest = jnp.full((8, 256), -3e38, F32)
    empty = jnp.zeros((128, 256), F32)

    def set_top(slot, top):
        tops[slot] = jnp.broadcast_to(jnp.max(top, axis=0, keepdims=True), (8, 256))

    def copy_out(block, slot):
        return pltpu.make_async_copy(weights.at[slot], probs_ref.at[block], out_sems.at[slot])

    def finish(block, slot, total):
        inverse = 1.0 / total[96:97]
        mean = total[0:96] * inverse
        for n in range(2):
            lanes = slice(n * TILE, (n + 1) * TILE)
            att_ref[2 * block + n] = mean[:, lanes].astype(BF16)
            mean_ref[2 * block + n, 0:96, :] = mean[:, lanes]
            mean_ref[2 * block + n, 96:104, :] = jnp.broadcast_to(inverse[:, lanes], (8, TILE))
        copy_out(block, slot).start()

    first = lax.fori_loop(0, 8, lambda step, top: score(0, 0, step, top), lowest)
    set_top(0, first)

    def both(block, carry):
        now, later = lax.rem(block, 2), lax.rem(block + 1, 2)
        top_now = tops[now, 0:1, :]

        @pl.when(block >= 2)
        def _():
            copy_out(block, now).wait()

        def step_both(step, state):
            top, total = state
            top = score(block + 1, later, step, top)
            total = weigh(block, now, step, top_now, total, False)
            return top, total

        top, total = lax.fori_loop(0, 7, step_both, (lowest, empty))
        top = score(block + 1, later, 7, top)
        total = weigh(block, now, 7, top_now, total, True)
        set_top(later, top)
        finish(block, now, total)
        return carry

    lax.fori_loop(0, 7, both, 0)
    copy_out(7, 1).wait()
    top_now = tops[1, 0:1, :]
    total = lax.fori_loop(
        0, 7, lambda step, total: weigh(7, 1, step, top_now, total, False), empty
    )
    total = weigh(7, 1, 7, top_now, total, True)
    finish(7, 1, total)
    copy_out(6, 0).wait()
    copy_out(7, 1).wait()


def attend_forward(slopes, lengths, qt, kvt):
    return pl.pallas_call(
        forward_kernel,
        out_shape=(
            jax.ShapeDtypeStruct((16, 96, 128), BF16),
            jax.ShapeDtypeStruct((16, 104, 128), F32),
            jax.ShapeDtypeStruct((8, 8, 512, 256), BF16),
        ),
        in_specs=[IN_SMEM, IN_SMEM, IN_VMEM, IN_VMEM],
        out_specs=[IN_VMEM, IN_VMEM, ANY],
        scratch_shapes=[
            pltpu.VMEM((4096, 256), BF16),
            pltpu.VMEM((8, 128, 512), BF16),
            pltpu.VMEM((8, 2, 256, 256), BF16),
            pltpu.VMEM((2, 4096, 256), F32),
            pltpu.VMEM((2, 8, 512, 256), BF16),
            pltpu.VMEM((2, 8, 256), F32),
            pltpu.SemaphoreType.DMA((2,)),
        ],
        compiler_params=pltpu.CompilerParams(vmem_limit_bytes=VMEM_BYTES),
        name="attend_forward",
    )(slopes, lengths, qt, kvt)


def shifted_rows(x, shift):
    return x if shift == 0 else pltpu.roll(x, 160 - shift, 0)


def middle_kernel(
    lengths_ref, att_ref, resid_ref, cot_ref, w_ref, taps_ref,
    block_out, resid_out, dot_ref, weight_ref,
    att_t, att_sibling, att_rows, stream, padded, grad_padded, block_rows, grad_rows, grad_pair,
    grad_heads, kernel_rows, product,
    att_send, att_recv, fwd_send, fwd_recv, halo_send, halo_recv, dot_send, dot_recv,
    pair_send, pair_recv, out_send, out_recv, out_local, keep_local,
):
    me = lax.axis_index("ctx")
    core, chip = lax.rem(me, 2), me // 2
    sibling = me + 1 - 2 * core
    half, place = chip // 16, lax.rem(chip, 16)
    barrier_all(me, 64)
    send_heads(me, att_ref, att_t, place, half, att_send, att_recv.at[place])

    def forward(step, carry):
        head = lax.rem(step + chip, 16)
        arrived(att_t.at[head], att_recv.at[head])
        remote(
            att_t.at[head], att_sibling.at[head], fwd_send.at[head], fwd_recv.at[head], ctx=sibling
        ).start()
        return carry

    lax.fori_loop(0, 16, forward, 0)
    for t in range(12):
        pieces = []
        for u in range(4):
            feature = t * TILE + u * 32
            pieces.append(att_t[feature // 96, feature % 96 : feature % 96 + 32, :])
        tile = jnp.concatenate(pieces, axis=0)
        att_rows[:, t * TILE : (t + 1) * TILE] = tile.T

    length = lengths_ref[core]
    frame = chip * TILE + lax.broadcasted_iota(jnp.int32, (TILE, TILE), 0)
    live = frame < length

    def project(j, carry):
        lanes = pl.ds(pl.multiple_of(j * 256, 256), 256)
        mixed = jnp.dot(att_rows[...], w_ref[:, lanes], preferred_element_type=F32)
        total = (resid_ref[:, lanes].astype(F32) + mixed).astype(BF16)
        stream[:, lanes] = total
        wide = jnp.concatenate([live, live], axis=1)
        padded[16:144, lanes] = jnp.where(wide, total, jnp.zeros_like(total))
        return carry

    lax.fori_loop(0, 6, project, 0)

    def halo(buffer, n):
        up = remote(
            buffer.at[pl.ds(128, 16)], buffer.at[pl.ds(0, 16)],
            halo_send.at[n], halo_recv.at[n], ctx=jnp.minimum(me + 2, 63),
        )
        down = remote(
            buffer.at[pl.ds(16, 16)], buffer.at[pl.ds(144, 16)],
            halo_send.at[n + 1], halo_recv.at[n + 1], ctx=jnp.maximum(me - 2, 0),
        )
        return up, down

    def halo_start(buffer, n):
        up, down = halo(buffer, n)

        @pl.when(chip < 31)
        def _():
            up.start()

        @pl.when(chip > 0)
        def _():
            down.start()

        edge = jnp.zeros((16, 1536), BF16)

        @pl.when(chip == 0)
        def _():
            buffer[0:16, :] = edge

        @pl.when(chip == 31)
        def _():
            buffer[144:160, :] = edge

    def halo_wait(buffer, n):
        up, down = halo(buffer, n)

        @pl.when(chip > 0)
        def _():
            up.wait_recv()

        @pl.when(chip < 31)
        def _():
            down.wait_recv()

    def halo_sent(buffer, n):
        up, down = halo(buffer, n)

        @pl.when(chip < 31)
        def _():
            up.wait_send()

        @pl.when(chip > 0)
        def _():
            down.wait_send()

    halo_start(padded, 0)
    kernel_rows[...] = jnp.zeros_like(kernel_rows)
    halo_wait(padded, 0)

    def lanes_of(j):
        return pl.ds(pl.multiple_of(j * TILE, TILE), TILE)

    def convolve(j, carry):
        lanes = lanes_of(j)
        taps = taps_ref[:, lanes]
        x = padded[:, lanes].astype(F32)
        conv = jnp.zeros((TILE, TILE), F32)
        for shift in range(8):
            moved = shifted_rows(x, shift)
            for m in range(4):
                tap = 8 * m + shift - 1
                if tap >= 0:
                    conv = conv + taps[tap : tap + 1] * moved[8 * m : 8 * m + TILE]
        squash = 1.0 / (1.0 + jnp.exp(-conv))
        block_rows[:, lanes] = (stream[:, lanes].astype(F32) + conv * squash).astype(BF16)
        cot = cot_ref[:, lanes].astype(F32)
        grad_padded[16:144, lanes] = (cot * squash * (1.0 + conv * (1.0 - squash))).astype(BF16)
        return carry

    lax.fori_loop(0, 12, convolve, 0)
    halo_start(grad_padded, 2)
    mine = pl.ds(pl.multiple_of(core * 64, 64), 64)
    other = pl.ds(pl.multiple_of((1 - core) * 64, 64), 64)
    block_there = remote(
        block_rows.at[other], block_out.at[core], out_send.at[0], out_recv.at[0], ctx=sibling
    )
    block_there.start()
    block_here = pltpu.make_async_copy(block_rows.at[mine], block_out.at[core], out_local.at[0])
    block_here.start()

    def kernel_grad(j, carry):
        lanes = lanes_of(j)
        x = padded[:, lanes].astype(F32)
        grad = grad_padded[16:144, lanes].astype(F32)
        for shift in range(8):
            moved = shifted_rows(x, shift)
            for m in range(4):
                tap = 8 * m + shift - 1
                if tap >= 0:
                    kernel_rows[tap : tap + 1, lanes] = jnp.sum(
                        grad * moved[8 * m : 8 * m + TILE], axis=0, keepdims=True
                    )
        return carry

    lax.fori_loop(0, 12, kernel_grad, 0)
    halo_wait(grad_padded, 2)

    def back(j, carry):
        lanes = lanes_of(j)
        taps = taps_ref[:, lanes]
        x = grad_padded[:, lanes].astype(F32)
        conv = jnp.zeros((TILE, TILE), F32)
        for shift in range(8):
            moved = shifted_rows(x, shift)
            for m in range(4):
                tap = 31 - (8 * m + shift)
                if 0 <= tap < 31:
                    conv = conv + taps[tap : tap + 1] * moved[8 * m : 8 * m + TILE]
        total = cot_ref[:, lanes].astype(F32) + jnp.where(live, conv, 0.0)
        grad_rows[:, lanes] = total.astype(BF16)
        return carry

    lax.fori_loop(0, 12, back, 0)
    own_half = pl.ds(pl.multiple_of(core * 768, 768), 768)
    other_half = pl.ds(pl.multiple_of((1 - core) * 768, 768), 768)
    pair_there = remote(
        grad_rows.at[:, other_half], grad_pair.at[pl.ds(128, 128)],
        pair_send.at[0], pair_recv.at[0], ctx=sibling,
    )
    pair_there.start()
    pair_here = pltpu.make_async_copy(
        grad_rows.at[:, own_half], grad_pair.at[pl.ds(0, 128)], keep_local.at[0]
    )
    pair_here.start()
    resid_there = remote(
        grad_rows.at[other], resid_out.at[core], out_send.at[1], out_recv.at[1], ctx=sibling
    )
    resid_there.start()
    resid_here = pltpu.make_async_copy(grad_rows.at[mine], resid_out.at[core], out_local.at[1])
    resid_here.start()

    def unproject(head, carry):
        rows = pl.ds(pl.multiple_of(head * 96, 96), 96)
        grad_heads[head] = lax.dot_general(
            w_ref[rows, :], grad_rows[...], (((1,), (1,)), ((), ())), preferred_element_type=F32
        ).astype(BF16)
        return carry

    lax.fori_loop(0, 16, unproject, 0)
    send_heads(me, grad_heads, dot_ref, place, half, dot_send, dot_recv.at[place])

    def sibling_arrived(head, carry):
        arrived(att_sibling.at[head], fwd_recv.at[head])
        arrived(att_t.at[head], fwd_send.at[head])
        return carry

    lax.fori_loop(0, 16, sibling_arrived, 0)
    pair_here.wait()
    pair_there.wait_recv()

    def weight_grad(head, carry):
        both = jnp.concatenate([att_t[head], att_sibling[head]], axis=1)
        rows = pl.ds(pl.multiple_of(head * 96, 96), 96)
        product[rows, 0:768] = jnp.dot(
            both, grad_pair[...], preferred_element_type=F32
        ).astype(BF16)
        return carry

    lax.fori_loop(0, 16, weight_grad, 0)
    for t in range(12):
        product[t * TILE : (t + 1) * TILE, 768:896] = (
            kernel_rows[:, t * TILE : (t + 1) * TILE].T.astype(BF16)
        )
    keep = pltpu.make_async_copy(product, weight_ref, keep_local.at[1])
    keep.start()

    def dot_arrived(step, carry):
        arrived(dot_ref.at[step], dot_recv.at[step])
        return carry

    lax.fori_loop(0, 16, dot_arrived, 0)
    heads_sent(me, att_ref, half, att_send)
    heads_sent(me, grad_heads, half, dot_send)
    halo_sent(padded, 0)
    halo_sent(grad_padded, 2)
    pair_there.wait_send()
    for there, here in ((block_there, block_here), (resid_there, resid_here)):
        here.wait()
        there.wait_send()
        there.wait_recv()
    keep.wait()


def middle(lengths, att, resid, cotangent, w_out, taps):
    dma = pltpu.SemaphoreType.DMA
    return pl.pallas_call(
        middle_kernel,
        out_shape=(
            jax.ShapeDtypeStruct((2, 64, 1536), BF16),
            jax.ShapeDtypeStruct((2, 64, 1536), BF16),
            jax.ShapeDtypeStruct((16, 96, 128), BF16),
            jax.ShapeDtypeStruct((1536, 896), BF16),
        ),
        in_specs=[IN_SMEM] + [IN_VMEM] * 5,
        out_specs=[ANY] * 4,
        scratch_shapes=[
            pltpu.VMEM((16, 96, 128), BF16),
            pltpu.VMEM((16, 96, 128), BF16),
            pltpu.VMEM((128, 1536), BF16),
            pltpu.VMEM((128, 1536), BF16),
            pltpu.VMEM((160, 1536), BF16),
            pltpu.VMEM((160, 1536), BF16),
            pltpu.VMEM((128, 1536), BF16),
            pltpu.VMEM((128, 1536), BF16),
            pltpu.VMEM((256, 768), BF16),
            pltpu.VMEM((16, 96, 128), BF16),
            pltpu.VMEM((128, 1536), F32),
            pltpu.VMEM((1536, 896), BF16),
            dma((16,)), dma((16,)), dma((16,)), dma((16,)), dma((4,)), dma((4,)),
            dma((16,)), dma((16,)), dma((1,)), dma((1,)), dma((2,)), dma((2,)), dma((2,)),
            dma((2,)),
        ],
        compiler_params=pltpu.CompilerParams(
            collective_id=1, has_side_effects=True, vmem_limit_bytes=VMEM_BYTES
        ),
        name="middle",
    )(lengths, att, resid, cotangent, w_out, taps)


def backward_kernel(
    qt_ref, kvt_ref, dot_ref, mean_ref, probs_ref, weight_ref,
    gq_out, gk_out, gv_out, gw_out, taps_out,
    values, key_cols, dot_cols, dot_rows, query_rows_ref, weights, sum_k, sum_v, sum_q,
    part_mine, part_sent, part_got, back_kv, back_q, got_kv, got_q, final,
    shares, share_sum, share_send, share_got, total_ref, pair_got,
    probs_sems, ws_send, ws_recv, part_send, part_recv, kv_send, kv_recv, q_send, q_recv,
    group_send, group_recv, pair_send, pair_recv, out_send, out_recv, out_local,
):
    me = lax.axis_index("ctx")
    group = lax.axis_index("dp")
    core, chip = lax.rem(me, 2), me // 2
    sibling = me + 1 - 2 * core
    half, place = chip // 16, lax.rem(chip, 16)
    barrier_all(me, 64, 4)

    def send_share(step, carry):
        to = lax.rem(chip + step, 32)
        rows = pl.ds(pl.multiple_of(to * 48, 48), 48)
        send_block(
            me, to * 2 + core, weight_ref.at[rows], shares.at[chip], ws_send.at[to], ws_recv.at[chip]
        )
        return carry

    lax.fori_loop(0, 32, send_share, 0)

    def fetch(chunk, slot):
        return pltpu.make_async_copy(probs_ref.at[:, chunk], weights.at[slot], probs_sems.at[slot])

    fetch(0, 0).start()

    def build_keys(tile, carry):
        one = lax.broadcasted_iota(jnp.int32, (32, TILE), 0) < 3
        ones = jnp.where(one, 1.0, 0.0).astype(BF16)
        wide = jnp.concatenate([kvt_ref[tile, 96:192, :], ones], axis=0)
        values[pl.ds(pl.multiple_of(tile * TILE, TILE), TILE), :] = wide.T
        lanes = pl.ds(pl.multiple_of(lax.rem(tile, 4) * TILE, TILE), TILE)
        key_cols[tile // 4, :, lanes] = kvt_ref[tile, 0:96, :]
        return carry

    lax.fori_loop(0, 32, build_keys, 0)

    def build_queries(tile, carry):
        mean = mean_ref[tile, 0:96, :]
        inverse = mean_ref[tile, 96:97, :]
        scaled = (dot_ref[tile].astype(F32) * inverse).astype(BF16)
        row_dot = jnp.sum(scaled.astype(F32) * mean, axis=0, keepdims=True)
        parts = three_parts(row_dot)
        row = lax.broadcasted_iota(jnp.int32, (32, TILE), 0)
        extra = jnp.zeros((32, TILE), F32)
        for n in range(3):
            extra = jnp.where(row == n, -parts[n], extra)
        wide = jnp.concatenate([scaled, extra.astype(BF16)], axis=0)
        lanes = pl.ds(pl.multiple_of(lax.rem(tile, 2) * TILE, TILE), TILE)
        rows = pl.ds(pl.multiple_of(tile * TILE, TILE), TILE)
        dot_cols[tile // 2, :, lanes] = wide
        dot_rows[rows, :] = wide.T
        query = jnp.concatenate([qt_ref[tile], jnp.zeros((32, TILE), BF16)], axis=0)
        query_rows_ref[rows, :] = query.T
        return carry

    lax.fori_loop(0, 16, build_queries, 0)
    sum_q[...] = jnp.zeros_like(sum_q)

    def send_back(chunk):
        for n in range(2):
            index = 2 * chunk + n
            arrived(part_got.at[index], part_recv.at[index])
            total = part_mine[index] + part_got[index].astype(F32)
            back_kv[index] = total.astype(BF16)
            send_block(
                me, (2 * index + core) * 2 + half, back_kv.at[index], got_kv.at[place],
                kv_send.at[index], kv_recv.at[place],
            )

    def per_chunk(chunk, carry):
        slot = lax.rem(chunk, 2)
        fetch(chunk, slot).wait()

        @pl.when(chunk < 7)
        def _():
            fetch(chunk + 1, 1 - slot).start()

        rows = pl.ds(pl.multiple_of(chunk * 512, 512), 512)
        sum_k[...] = jnp.zeros_like(sum_k)
        sum_v[...] = jnp.zeros_like(sum_v)

        def per_block(block, inner):
            places = pl.ds(pl.multiple_of(block * 256, 256), 256)
            weight = weights[slot, block]
            dprob = jnp.dot(values[rows, :], dot_cols[block], preferred_element_type=F32)
            dscore = (weight.astype(F32) * dprob).astype(BF16)
            sum_v[...] += jnp.dot(weight, dot_rows[places, :], preferred_element_type=F32)
            sum_k[...] += jnp.dot(dscore, query_rows_ref[places, :], preferred_element_type=F32)
            sum_q[block] += jnp.dot(key_cols[chunk], dscore, preferred_element_type=F32)
            return inner

        lax.fori_loop(0, 8, per_block, 0)

        @pl.when(chunk > 0)
        def _():
            send_back(chunk - 1)

        for n in range(2):
            index = 2 * chunk + n
            for kind, sums, factor in ((0, sum_k, SCALE), (1, sum_v, 1.0)):
                first = pl.ds(pl.multiple_of((2 * n + core) * TILE, TILE), TILE)
                second = pl.ds(pl.multiple_of((2 * n + 1 - core) * TILE, TILE), TILE)
                features = slice(kind * 96, kind * 96 + 96)
                part_mine[index, features, :] = sums[first, :].T[0:96] * factor
                part_sent[index, features, :] = (sums[second, :].T[0:96] * factor).astype(BF16)
            remote(
                part_sent.at[index], part_got.at[index], part_send.at[index], part_recv.at[index],
                ctx=sibling,
            ).start()
        return carry

    lax.fori_loop(0, 8, per_chunk, 0)

    def finish_queries(block, carry):
        for n in range(2):
            back_q[2 * block + n] = (
                sum_q[block, :, n * TILE : (n + 1) * TILE] * SCALE
            ).astype(BF16)
        return carry

    lax.fori_loop(0, 8, finish_queries, 0)
    send_heads(me, back_q, got_q, place, half, q_send, q_recv.at[place])
    send_back(7)

    share_sum[...] = jnp.zeros_like(share_sum)

    def add_share(step, carry):
        slot = lax.rem(chip + step, 32)
        arrived(shares.at[slot], ws_recv.at[slot])
        share_sum[...] += shares[slot].astype(F32)
        return carry

    lax.fori_loop(0, 32, add_share, 0)
    share_send[...] = share_sum[...].astype(BF16)
    for step in range(1, 4):
        remote(
            share_send, share_got.at[step - 1], group_send.at[step - 1], group_recv.at[step - 1],
            dp=lax.rem(group + step, 4),
        ).start()

    def tile_back(n, t):
        pieces = []
        for u in range(4):
            feature = t * TILE + u * 32
            head, first = feature // 96, feature % 96
            if n == 0:
                pieces.append(got_q[head, first : first + 32, :])
            else:
                first = first + (n - 1) * 96
                pieces.append(got_kv[head, first : first + 32, :])
        final[n, :, t * TILE : (t + 1) * TILE] = jnp.concatenate(pieces, axis=0).T

    mine = pl.ds(pl.multiple_of(core * 64, 64), 64)
    other = pl.ds(pl.multiple_of((1 - core) * 64, 64), 64)
    outs = (gq_out, gk_out, gv_out)

    def out_copies(n):
        there = remote(
            final.at[n, other], outs[n].at[core], out_send.at[n], out_recv.at[n], ctx=sibling
        )
        here = pltpu.make_async_copy(final.at[n, mine], outs[n].at[core], out_local.at[n])
        return there, here

    def kv_arrived(step, carry):
        arrived(got_kv.at[step], kv_recv.at[step])
        return carry

    def q_arrived(step, carry):
        arrived(got_q.at[step], q_recv.at[step])
        return carry

    lax.fori_loop(0, 16, q_arrived, 0)
    for n in (0, 1, 2):
        if n == 1:
            lax.fori_loop(0, 16, kv_arrived, 0)
        for t in range(12):
            tile_back(n, t)
        there, here = out_copies(n)
        there.start()
        here.start()

    for step in range(3):
        arrived(share_got.at[step], group_recv.at[step])
        share_sum[...] += share_got[step].astype(F32)
    total_ref[...] = share_sum[...] * (1.0 / math.sqrt(32768))
    give = pl.ds(pl.multiple_of((1 - core) * 24, 8), 24)
    keep = pl.ds(pl.multiple_of(core * 24, 8), 24)
    pair = remote(total_ref.at[give], pair_got, pair_send.at[0], pair_recv.at[0], ctx=sibling)
    pair.start()
    pair.wait_recv()
    own_half = pl.ds(pl.multiple_of(core * 768, 768), 768)
    other_half = pl.ds(pl.multiple_of((1 - core) * 768, 768), 768)
    gw_out[:, own_half] = total_ref[keep, 0:768]
    gw_out[:, other_half] = pair_got[:, 0:768]
    taps_out[...] = total_ref[keep, 768:896] + pair_got[:, 768:896]

    pair.wait_send()
    for step in range(3):
        arrived(share_send, group_send.at[step])

    def all_sent(step, carry):
        @pl.when(step * 2 + core != me)
        def _():
            arrived(weight_ref.at[pl.ds(0, 48)], ws_send.at[step])

        return carry

    lax.fori_loop(0, 32, all_sent, 0)

    def parts_sent(step, carry):
        arrived(part_sent.at[step], part_send.at[step])

        @pl.when((2 * step + core) * 2 + half != me)
        def _():
            arrived(back_kv.at[step], kv_send.at[step])

        return carry

    lax.fori_loop(0, 16, parts_sent, 0)
    heads_sent(me, back_q, half, q_send)
    for n in range(3):
        there, here = out_copies(n)
        here.wait()
        there.wait_send()
        there.wait_recv()


def attend_backward(qt, kvt, dot, mean, probs, weight):
    dma = pltpu.SemaphoreType.DMA
    grads = jax.ShapeDtypeStruct((2, 64, 1536), BF16)
    return pl.pallas_call(
        backward_kernel,
        out_shape=(
            grads,
            grads,
            grads,
            jax.ShapeDtypeStruct((24, 1536), F32),
            jax.ShapeDtypeStruct((24, 128), F32),
        ),
        in_specs=[IN_VMEM] * 4 + [ANY] * 2,
        out_specs=[ANY] * 3 + [IN_VMEM] * 2,
        scratch_shapes=[
            pltpu.VMEM((4096, 128), BF16),
            pltpu.VMEM((8, 96, 512), BF16),
            pltpu.VMEM((8, 128, 256), BF16),
            pltpu.VMEM((2048, 128), BF16),
            pltpu.VMEM((2048, 128), BF16),
            pltpu.VMEM((2, 8, 512, 256), BF16),
            pltpu.VMEM((512, 128), F32),
            pltpu.VMEM((512, 128), F32),
            pltpu.VMEM((8, 96, 256), F32),
            pltpu.VMEM((16, 192, 128), F32),
            pltpu.VMEM((16, 192, 128), BF16),
            pltpu.VMEM((16, 192, 128), BF16),
            pltpu.VMEM((16, 192, 128), BF16),
            pltpu.VMEM((16, 96, 128), BF16),
            pltpu.VMEM((16, 192, 128), BF16),
            pltpu.VMEM((16, 96, 128), BF16),
            pltpu.VMEM((3, 128, 1536), BF16),
            pltpu.VMEM((32, 48, 896), BF16),
            pltpu.VMEM((48, 896), F32),
            pltpu.VMEM((48, 896), BF16),
            pltpu.VMEM((3, 48, 896), BF16),
            pltpu.VMEM((48, 896), F32),
            pltpu.VMEM((24, 896), F32),
            dma((2,)), dma((32,)), dma((32,)), dma((16,)), dma((16,)), dma((16,)), dma((16,)),
            dma((16,)), dma((16,)), dma((3,)), dma((3,)), dma((1,)), dma((1,)), dma((3,)),
            dma((3,)), dma((3,)),
        ],
        compiler_params=pltpu.CompilerParams(
            collective_id=2, has_side_effects=True, vmem_limit_bytes=VMEM_BYTES
        ),
        name="attend_backward",
    )(qt, kvt, dot, mean, probs, weight)


def per_device(resid, queries, keys_in, values, w_out, slopes, kernel, lengths, cotangent):
    qt, kvt, resid_rows, cot_rows = spread_heads(queries, keys_in, values, resid, cotangent)
    att, mean, probs = attend_forward(slopes, lengths, qt, kvt)
    block_out, grad_resid, dot, weight = middle(lengths, att, resid_rows, cot_rows, w_out, kernel)
    grad_q, grad_k, grad_v, grad_w, grad_taps = attend_backward(qt, kvt, dot, mean, probs, weight)
    grad_kernel = grad_taps[:, :31].T
    return (block_out, grad_resid, grad_q, grad_k, grad_v, grad_w, grad_kernel)


def solution(mesh):
    spread = P("dp", "ctx", None)
    in_specs = (spread, spread, spread, spread, P(), P(), P(), P("dp"), spread)
    out_specs = (spread, spread, spread, spread, spread, P("ctx", None), P(None, "ctx"))
    return jax.shard_map(
        per_device, mesh=mesh, in_specs=in_specs, out_specs=out_specs, check_vma=False
    )
```

```python
import math

import jax
import jax.numpy as jnp
from jax import lax
from jax.experimental import pallas as pl
from jax.experimental.pallas import tpu as pltpu
from jax.sharding import PartitionSpec as P

F32 = jnp.float32
BF16 = jnp.bfloat16
VMEM_BYTES = 56 * 1024 * 1024
ANY = pl.BlockSpec(memory_space=pl.ANY)
IN_VMEM = pl.BlockSpec(memory_space=pltpu.VMEM)
IN_SMEM = pl.BlockSpec(memory_space=pltpu.SMEM)
FRAMES = 4096
CHUNK = 2048
SCALE = 1.0 / math.sqrt(96)
LOG2E = math.log2(math.e)
MESH = pl.DeviceIdType.MESH
TILE = 128


def barrier_all(me, count, groups=1):
    barrier = pltpu.get_barrier_semaphore()
    here = lax.axis_index("dp")

    def greet(step, carry):
        other = lax.rem(me + step, count)
        pl.semaphore_signal(barrier, inc=1, device_id={"ctx": other}, device_id_type=MESH)
        return carry

    lax.fori_loop(1, count, greet, 0)
    for step in range(1, groups):
        other = lax.rem(here + step, groups)
        pl.semaphore_signal(barrier, inc=1, device_id={"dp": other}, device_id_type=MESH)
    pl.semaphore_wait(barrier, count + groups - 2)


def arrived(ref, sem):
    pltpu.make_async_copy(ref, ref, sem).wait()


def nth_head(chip, step):
    y = lax.rem(step // 8 + step // 2, 2)
    x = lax.rem(step // 2 + chip, 4)
    return y * 8 + lax.rem(step, 2) * 4 + x


def nth_chip(chip, core, step):
    turn = lax.rem(step + 16 * core, 32)
    ahead = lax.rem(turn // 2, 4)
    x = lax.rem(chip + ahead, 4)
    z = lax.rem(chip // 4 + turn, 2)
    y = lax.rem(chip // 8 + ahead + turn // 8, 4)
    return y * 8 + z * 4 + x

def send_heads(me, buffer, target, slot, target_core, send_sems, recv_sem):
    core, chip = lax.rem(me, 2), me // 2

    def one(step, carry):
        head = nth_head(chip, step)
        send_block(
            me,
            (core * 16 + head) * 2 + target_core,
            buffer.at[head],
            target.at[slot],
            send_sems.at[head],
            recv_sem,
        )
        return carry

    lax.fori_loop(0, 16, one, 0)


def send_block(me, other, source, target, send_sem, recv_sem):
    @pl.when(other != me)
    def _():
        pltpu.make_async_remote_copy(
            src_ref=source,
            dst_ref=target,
            send_sem=send_sem,
            recv_sem=recv_sem,
            device_id={"ctx": other},
            device_id_type=MESH,
        ).start()

    @pl.when(other == me)
    def _():
        pltpu.make_async_copy(source, target, recv_sem).start()


def heads_sent(me, buffer, target_core, send_sems):
    core = lax.rem(me, 2)

    def one(head, carry):
        other = (core * 16 + head) * 2 + target_core

        @pl.when(other != me)
        def _():
            arrived(buffer.at[head], send_sems.at[head])

        return carry

    lax.fori_loop(0, 16, one, 0)


def remote(source, target, send_sem, recv_sem, **device):
    return pltpu.make_async_remote_copy(
        src_ref=source,
        dst_ref=target,
        send_sem=send_sem,
        recv_sem=recv_sem,
        device_id=device,
        device_id_type=MESH,
    )


def spread_kernel(
    q_ref, k_ref, v_ref,
    qt_ref, kvt_ref,
    halves, send_q, send_kv,
    swap_send, swap_recv, swap_local, q_send, kv_send, q_recv, kv_recv, fwd_send,
):
    me = lax.axis_index("ctx")
    core = lax.rem(me, 2)
    chip = me // 2
    sibling = me + 1 - 2 * core
    barrier_all(me, 64)

    rows = pl.ds(pl.multiple_of(core * 64, 64), 64)
    sources = [q_ref, k_ref, v_ref]
    swaps = {}
    for n in (1, 2, 0):
        there = pltpu.make_async_remote_copy(
            src_ref=sources[n].at[1 - core],
            dst_ref=halves.at[n, rows],
            send_sem=swap_send.at[n],
            recv_sem=swap_recv.at[n],
            device_id={"ctx": sibling},
            device_id_type=MESH,
        )
        here = pltpu.make_async_copy(sources[n].at[core], halves.at[n, rows], swap_local.at[n])
        there.start()
        here.start()
        swaps[n] = (there, here)

    def turn(n):
        there, here = swaps[n]
        here.wait()
        there.wait_recv()
        for t in range(12):
            flipped = halves[n, :, t * TILE : (t + 1) * TILE].T
            for u in range(4):
                feature = t * TILE + u * 32
                head, place = feature // 96, feature % 96
                piece = flipped[u * 32 : (u + 1) * 32]
                if n == 0:
                    send_q[head, place : place + 32, :] = piece
                else:
                    first = place + (n - 1) * 96
                    send_kv[head, first : first + 32, :] = piece

    half = chip // 16
    parity = lax.rem(chip, 2)

    turn(1)
    turn(2)
    send_heads(me, send_kv, kvt_ref, chip, parity, kv_send, kv_recv.at[chip])
    turn(0)
    place = lax.rem(chip, 16)
    send_heads(me, send_q, qt_ref, place, half, q_send, q_recv.at[place])

    def forward(step, carry):
        slot = 2 * lax.rem(step + chip // 2, 16) + core
        arrived(kvt_ref.at[slot], kv_recv.at[slot])
        pltpu.make_async_remote_copy(
            src_ref=kvt_ref.at[slot],
            dst_ref=kvt_ref.at[slot],
            send_sem=fwd_send.at[slot // 2],
            recv_sem=kv_recv.at[slot],
            device_id={"ctx": sibling},
            device_id_type=MESH,
        ).start()
        return carry

    lax.fori_loop(0, 16, forward, 0)

    def finish(step, carry):
        arrived(qt_ref.at[step], q_recv.at[step])
        other = 2 * step + 1 - core
        arrived(kvt_ref.at[other], kv_recv.at[other])
        mine = 2 * step + core
        arrived(kvt_ref.at[mine], fwd_send.at[step])
        return carry

    lax.fori_loop(0, 16, finish, 0)
    heads_sent(me, send_kv, parity, kv_send)
    heads_sent(me, send_q, half, q_send)
    for n in (1, 2, 0):
        there, here = swaps[n]
        there.wait_send()


def spread_heads(queries, keys_in, values):
    bf16 = jnp.bfloat16
    any_space = pl.BlockSpec(memory_space=pl.ANY)
    return pl.pallas_call(
        spread_kernel,
        out_shape=(
            jax.ShapeDtypeStruct((16, 96, 128), bf16),
            jax.ShapeDtypeStruct((32, 192, 128), bf16),
        ),
        in_specs=[any_space] * 3,
        out_specs=[any_space] * 2,
        scratch_shapes=[
            pltpu.VMEM((3, 128, 1536), bf16),
            pltpu.VMEM((16, 96, 128), bf16),
            pltpu.VMEM((16, 192, 128), bf16),
            pltpu.SemaphoreType.DMA((3,)),
            pltpu.SemaphoreType.DMA((3,)),
            pltpu.SemaphoreType.DMA((3,)),
            pltpu.SemaphoreType.DMA((16,)),
            pltpu.SemaphoreType.DMA((16,)),
            pltpu.SemaphoreType.DMA((16,)),
            pltpu.SemaphoreType.DMA((32,)),
            pltpu.SemaphoreType.DMA((16,)),
        ],
        compiler_params=pltpu.CompilerParams(collective_id=0, has_side_effects=True),
        name="spread_heads",
    )(queries, keys_in, values)


def three_parts(value):
    first = value.astype(BF16).astype(F32)
    second = (value - first).astype(BF16).astype(F32)
    return first, second, value - first - second


def key_rows(tile, length):
    row = lax.broadcasted_iota(jnp.int32, (64, TILE), 0)
    frame = tile * TILE + lax.broadcasted_iota(jnp.int32, (64, TILE), 1)
    low = lax.rem(frame, 64)
    hidden = jnp.where((frame >= length) & (row == 9), -1e30, 0.0)
    place = jnp.where(lax.rem(row, 2) == 0, frame - low, low).astype(F32)
    signed = jnp.where(row < 6, place, jnp.where(row < 9, 1.0, 0.0))
    return (hidden + signed).astype(BF16), (hidden - signed).astype(BF16)


def query_rows(first_frame, rate):
    row = lax.broadcasted_iota(jnp.int32, (64, TILE), 0)
    frame = first_frame + lax.broadcasted_iota(jnp.int32, (64, TILE), 1)
    rates = three_parts(jnp.full((64, TILE), rate, F32))
    shifts = three_parts(rate * frame.astype(F32))
    rows = jnp.where(row == 9, 1.0, 0.0)
    for n in range(3):
        rows = jnp.where(row // 2 == n, rates[n], rows)
        rows = jnp.where(row == 6 + n, -shifts[n], rows)
    return rows.astype(BF16)


def forward_kernel(
    slopes_ref, lengths_ref, qt_ref, kvt_ref,
    att_ref, mean_ref, probs_ref,
    keys, value_rows, query_cols, scores, weights, tops, out_sems,
):
    me = lax.axis_index("ctx")
    core, chip = lax.rem(me, 2), me // 2
    rate = slopes_ref[lax.rem(chip, 16)] * (LOG2E / FRAMES)
    length = lengths_ref[chip // 16]

    def build_keys(tile, carry):
        kt = kvt_ref[tile, 0:96, :]
        before, after = key_rows(tile, length)
        rows = pl.ds(pl.multiple_of(tile * TILE, TILE), TILE)
        keys[0, rows, :] = jnp.concatenate([kt, kt, before], axis=0).T
        keys[1, rows, :] = jnp.concatenate([kt, kt, after], axis=0).T
        per = CHUNK // TILE
        lanes = pl.ds(pl.multiple_of(lax.rem(tile, per) * TILE, TILE), TILE)
        one = lax.broadcasted_iota(jnp.int32, (32, TILE), 0) == 0
        value_rows[tile // per, 0:96, lanes] = kvt_ref[tile, 96:192, :]
        value_rows[tile // per, 96:128, lanes] = jnp.where(one, 1.0, 0.0).astype(BF16)
        return carry

    lax.fori_loop(0, 32, build_keys, 0)

    def build_queries(tile, carry):
        scaled = qt_ref[tile].astype(F32) * (SCALE * LOG2E)
        high = scaled.astype(BF16)
        low = (scaled - high.astype(F32)).astype(BF16)
        extra = query_rows(core * 2048 + tile * TILE, rate)
        lanes = pl.ds(pl.multiple_of(lax.rem(tile, 2) * TILE, TILE), TILE)
        query_cols[tile // 2, :, lanes] = jnp.concatenate([high, low, extra], axis=0)
        return carry

    lax.fori_loop(0, 16, build_queries, 0)

    def chunk_rows(chunk):
        return pl.ds(pl.multiple_of(chunk * CHUNK, CHUNK), CHUNK)

    def score(block, slot, chunk, top):
        pieces = []
        for n in range(CHUNK // 256):
            part = chunk * (CHUNK // 256) + n
            side = jnp.where(part > core * 8 + block, 1, 0)
            pieces.append(keys[side, pl.ds(pl.multiple_of(part * 256, 256), 256), :])
        result = jnp.dot(
            jnp.concatenate(pieces, axis=0), query_cols[block], preferred_element_type=F32
        )
        scores[slot, chunk_rows(chunk), :] = result
        return jnp.maximum(top, jnp.max(result.reshape(CHUNK // 8, 8, 256), axis=0))

    def scored(block, slot, top):
        tops[slot] = jnp.broadcast_to(jnp.max(top, axis=0, keepdims=True), (8, 256))
        rows = pl.ds(pl.multiple_of((core * 8 + block) * 256, 256), 256)
        key = lax.broadcasted_iota(jnp.int32, (256, 256), 0)
        query = lax.broadcasted_iota(jnp.int32, (256, 256), 1)
        ahead = jnp.maximum(key - query, 0).astype(F32)
        scores[slot, rows, :] = scores[slot, rows, :] - (2.0 * rate) * ahead

    def weigh(slot, chunk, top, total):
        weight = jnp.exp2(scores[slot, chunk_rows(chunk), :] - top).astype(BF16)
        weights[slot, chunk_rows(chunk), :] = weight
        return total + jnp.dot(value_rows[chunk], weight, preferred_element_type=F32)

    lowest = jnp.full((8, 256), -3e38, F32)
    empty = jnp.zeros((128, 256), F32)

    def copy_out(block, slot):
        lanes = pl.ds(pl.multiple_of(block * 256, 256), 256)
        return pltpu.make_async_copy(weights.at[slot], probs_ref.at[:, lanes], out_sems.at[slot])

    def finish(block, slot, total):
        inverse = 1.0 / total[96:97]
        mean = total[0:96] * inverse
        for n in range(2):
            lanes = slice(n * TILE, (n + 1) * TILE)
            att_ref[2 * block + n] = mean[:, lanes].astype(BF16)
            mean_ref[2 * block + n, 0:96, :] = mean[:, lanes]
            mean_ref[2 * block + n, 96:104, :] = jnp.broadcast_to(inverse[:, lanes], (8, TILE))
        copy_out(block, slot).start()

    count = FRAMES // CHUNK
    first = lax.fori_loop(0, count, lambda chunk, top: score(0, 0, chunk, top), lowest)
    scored(0, 0, first)

    def both(block, carry):
        now, later = lax.rem(block, 2), lax.rem(block + 1, 2)
        top_now = tops[now, 0:1, :]

        @pl.when(block >= 2)
        def _():
            copy_out(block, now).wait()

        def step_both(chunk, state):
            top, total = state
            top = score(block + 1, later, chunk, top)
            total = weigh(now, chunk, top_now, total)
            return top, total

        top, total = lax.fori_loop(0, count, step_both, (lowest, empty))
        scored(block + 1, later, top)
        finish(block, now, total)
        return carry

    lax.fori_loop(0, 7, both, 0)
    copy_out(7, 1).wait()
    top_now = tops[1, 0:1, :]
    total = lax.fori_loop(
        0, count, lambda chunk, total: weigh(1, chunk, top_now, total), empty
    )
    finish(7, 1, total)
    copy_out(6, 0).wait()
    copy_out(7, 1).wait()


def attend_forward(slopes, lengths, qt, kvt):
    return pl.pallas_call(
        forward_kernel,
        out_shape=(
            jax.ShapeDtypeStruct((16, 96, 128), BF16),
            jax.ShapeDtypeStruct((16, 104, 128), F32),
            jax.ShapeDtypeStruct((4096, 2048), BF16),
        ),
        in_specs=[IN_SMEM, IN_SMEM, IN_VMEM, IN_VMEM],
        out_specs=[IN_VMEM, IN_VMEM, ANY],
        scratch_shapes=[
            pltpu.VMEM((2, 4096, 256), BF16),
            pltpu.VMEM((FRAMES // CHUNK, 128, CHUNK), BF16),
            pltpu.VMEM((8, 256, 256), BF16),
            pltpu.VMEM((2, 4096, 256), F32),
            pltpu.VMEM((2, 4096, 256), BF16),
            pltpu.VMEM((2, 8, 256), F32),
            pltpu.SemaphoreType.DMA((2,)),
        ],
        compiler_params=pltpu.CompilerParams(vmem_limit_bytes=VMEM_BYTES),
        name="attend_forward",
    )(slopes, lengths, qt, kvt)


def shifted_rows(x, shift):
    return x if shift == 0 else pltpu.roll(x, 160 - shift, 0)


def middle_kernel(
    lengths_ref, att_ref, resid_in, cot_in, w_ref, taps_ref,
    block_out, resid_out, dot_ref, weight_ref,
    resid_ref, cot_ref, att_t, att_sibling, att_rows, stream, padded, grad_padded, block_rows, grad_rows, grad_pair,
    grad_heads, kernel_rows, product,
    swap_send, swap_recv, att_send, att_recv, fwd_send, fwd_recv, halo_send, halo_recv, dot_send, dot_recv,
    pair_send, pair_recv, out_send, out_recv, out_local, keep_local,
):
    me = lax.axis_index("ctx")
    core, chip = lax.rem(me, 2), me // 2
    sibling = me + 1 - 2 * core
    half, place = chip // 16, lax.rem(chip, 16)
    barrier_all(me, 64)
    send_heads(me, att_ref, att_t, place, half, att_send, att_recv.at[place])
    mine = pl.ds(pl.multiple_of(core * 64, 64), 64)
    other = pl.ds(pl.multiple_of((1 - core) * 64, 64), 64)
    swaps = []
    for n, (source, target) in enumerate(((resid_in, resid_ref), (cot_in, cot_ref))):
        swap = remote(
            source.at[1 - core], target.at[mine], swap_send.at[n], swap_recv.at[n], ctx=sibling
        )
        swap.start()
        swaps.append(swap)
        target[mine, :] = source[core]

    def forward(step, carry):
        head = nth_head(chip, step)
        arrived(att_t.at[head], att_recv.at[head])
        remote(
            att_t.at[head], att_sibling.at[head], fwd_send.at[head], fwd_recv.at[head], ctx=sibling
        ).start()
        return carry

    lax.fori_loop(0, 16, forward, 0)
    for t in range(12):
        pieces = []
        for u in range(4):
            feature = t * TILE + u * 32
            pieces.append(att_t[feature // 96, feature % 96 : feature % 96 + 32, :])
        tile = jnp.concatenate(pieces, axis=0)
        att_rows[:, t * TILE : (t + 1) * TILE] = tile.T

    for swap in swaps:
        swap.wait()
    length = lengths_ref[core]
    frame = chip * TILE + lax.broadcasted_iota(jnp.int32, (TILE, TILE), 0)
    live = frame < length

    def project(j, carry):
        lanes = pl.ds(pl.multiple_of(j * 256, 256), 256)
        mixed = jnp.dot(att_rows[...], w_ref[:, lanes], preferred_element_type=F32)
        total = (resid_ref[:, lanes].astype(F32) + mixed).astype(BF16)
        stream[:, lanes] = total
        wide = jnp.concatenate([live, live], axis=1)
        padded[16:144, lanes] = jnp.where(wide, total, jnp.zeros_like(total))
        return carry

    lax.fori_loop(0, 6, project, 0)

    def halo(buffer, n):
        up = remote(
            buffer.at[pl.ds(128, 16)], buffer.at[pl.ds(0, 16)],
            halo_send.at[n], halo_recv.at[n], ctx=jnp.minimum(me + 2, 63),
        )
        down = remote(
            buffer.at[pl.ds(16, 16)], buffer.at[pl.ds(144, 16)],
            halo_send.at[n + 1], halo_recv.at[n + 1], ctx=jnp.maximum(me - 2, 0),
        )
        return up, down

    def halo_start(buffer, n):
        up, down = halo(buffer, n)

        @pl.when(chip < 31)
        def _():
            up.start()

        @pl.when(chip > 0)
        def _():
            down.start()

        edge = jnp.zeros((16, 1536), BF16)

        @pl.when(chip == 0)
        def _():
            buffer[0:16, :] = edge

        @pl.when(chip == 31)
        def _():
            buffer[144:160, :] = edge

    def halo_wait(buffer, n):
        up, down = halo(buffer, n)

        @pl.when(chip > 0)
        def _():
            up.wait_recv()

        @pl.when(chip < 31)
        def _():
            down.wait_recv()

    def halo_sent(buffer, n):
        up, down = halo(buffer, n)

        @pl.when(chip < 31)
        def _():
            up.wait_send()

        @pl.when(chip > 0)
        def _():
            down.wait_send()

    halo_start(padded, 0)
    kernel_rows[...] = jnp.zeros_like(kernel_rows)
    halo_wait(padded, 0)

    def lanes_of(j):
        return pl.ds(pl.multiple_of(j * TILE, TILE), TILE)

    def convolve(j, carry):
        lanes = lanes_of(j)
        taps = taps_ref[:, lanes]
        x = padded[:, lanes].astype(F32)
        conv = jnp.zeros((TILE, TILE), F32)
        for shift in range(8):
            moved = shifted_rows(x, shift)
            for m in range(4):
                tap = 8 * m + shift - 1
                if tap >= 0:
                    conv = conv + taps[tap : tap + 1] * moved[8 * m : 8 * m + TILE]
        squash = 1.0 / (1.0 + jnp.exp(-conv))
        block_rows[:, lanes] = (stream[:, lanes].astype(F32) + conv * squash).astype(BF16)
        cot = cot_ref[:, lanes].astype(F32)
        grad_padded[16:144, lanes] = (cot * squash * (1.0 + conv * (1.0 - squash))).astype(BF16)
        return carry

    lax.fori_loop(0, 12, convolve, 0)
    halo_start(grad_padded, 2)
    block_there = remote(
        block_rows.at[other], block_out.at[core], out_send.at[0], out_recv.at[0], ctx=sibling
    )
    block_there.start()
    block_here = pltpu.make_async_copy(block_rows.at[mine], block_out.at[core], out_local.at[0])
    block_here.start()

    def kernel_grad(j, carry):
        lanes = lanes_of(j)
        x = padded[:, lanes].astype(F32)
        grad = grad_padded[16:144, lanes].astype(F32)
        for shift in range(8):
            moved = shifted_rows(x, shift)
            for m in range(4):
                tap = 8 * m + shift - 1
                if tap >= 0:
                    kernel_rows[tap : tap + 1, lanes] = jnp.sum(
                        grad * moved[8 * m : 8 * m + TILE], axis=0, keepdims=True
                    )
        return carry

    lax.fori_loop(0, 12, kernel_grad, 0)
    halo_wait(grad_padded, 2)

    def back(j, carry):
        lanes = lanes_of(j)
        taps = taps_ref[:, lanes]
        x = grad_padded[:, lanes].astype(F32)
        conv = jnp.zeros((TILE, TILE), F32)
        for shift in range(8):
            moved = shifted_rows(x, shift)
            for m in range(4):
                tap = 31 - (8 * m + shift)
                if 0 <= tap < 31:
                    conv = conv + taps[tap : tap + 1] * moved[8 * m : 8 * m + TILE]
        total = cot_ref[:, lanes].astype(F32) + jnp.where(live, conv, 0.0)
        grad_rows[:, lanes] = total.astype(BF16)
        return carry

    lax.fori_loop(0, 12, back, 0)
    own_half = pl.ds(pl.multiple_of(core * 768, 768), 768)
    other_half = pl.ds(pl.multiple_of((1 - core) * 768, 768), 768)
    pair_there = remote(
        grad_rows.at[:, other_half], grad_pair.at[pl.ds(128, 128)],
        pair_send.at[0], pair_recv.at[0], ctx=sibling,
    )
    pair_there.start()
    pair_here = pltpu.make_async_copy(
        grad_rows.at[:, own_half], grad_pair.at[pl.ds(0, 128)], keep_local.at[0]
    )
    pair_here.start()
    resid_there = remote(
        grad_rows.at[other], resid_out.at[core], out_send.at[1], out_recv.at[1], ctx=sibling
    )
    resid_there.start()
    resid_here = pltpu.make_async_copy(grad_rows.at[mine], resid_out.at[core], out_local.at[1])
    resid_here.start()

    def unproject(head, carry):
        rows = pl.ds(pl.multiple_of(head * 96, 96), 96)
        grad_heads[head] = lax.dot_general(
            w_ref[rows, :], grad_rows[...], (((1,), (1,)), ((), ())), preferred_element_type=F32
        ).astype(BF16)
        return carry

    lax.fori_loop(0, 16, unproject, 0)
    send_heads(me, grad_heads, dot_ref, place, half, dot_send, dot_recv.at[place])

    def sibling_arrived(head, carry):
        arrived(att_sibling.at[head], fwd_recv.at[head])
        arrived(att_t.at[head], fwd_send.at[head])
        return carry

    lax.fori_loop(0, 16, sibling_arrived, 0)
    pair_here.wait()
    pair_there.wait_recv()

    def weight_grad(head, carry):
        both = jnp.concatenate([att_t[head], att_sibling[head]], axis=1)
        rows = pl.ds(pl.multiple_of(head * 96, 96), 96)
        product[rows, 0:768] = jnp.dot(
            both, grad_pair[...], preferred_element_type=F32
        ).astype(BF16)
        return carry

    lax.fori_loop(0, 16, weight_grad, 0)
    for t in range(12):
        product[t * TILE : (t + 1) * TILE, 768:896] = (
            kernel_rows[:, t * TILE : (t + 1) * TILE].T.astype(BF16)
        )
    keep = pltpu.make_async_copy(product, weight_ref, keep_local.at[1])
    keep.start()

    def dot_arrived(step, carry):
        arrived(dot_ref.at[step], dot_recv.at[step])
        return carry

    lax.fori_loop(0, 16, dot_arrived, 0)
    heads_sent(me, att_ref, half, att_send)
    heads_sent(me, grad_heads, half, dot_send)
    halo_sent(padded, 0)
    halo_sent(grad_padded, 2)
    pair_there.wait_send()
    for there, here in ((block_there, block_here), (resid_there, resid_here)):
        here.wait()
        there.wait_send()
        there.wait_recv()
    keep.wait()


def middle(lengths, att, resid, cotangent, w_out, taps):
    dma = pltpu.SemaphoreType.DMA
    return pl.pallas_call(
        middle_kernel,
        out_shape=(
            jax.ShapeDtypeStruct((2, 64, 1536), BF16),
            jax.ShapeDtypeStruct((2, 64, 1536), BF16),
            jax.ShapeDtypeStruct((16, 96, 128), BF16),
            jax.ShapeDtypeStruct((1536, 896), BF16),
        ),
        in_specs=[IN_SMEM] + [IN_VMEM] * 5,
        out_specs=[ANY] * 4,
        scratch_shapes=[
            pltpu.VMEM((128, 1536), BF16),
            pltpu.VMEM((128, 1536), BF16),
            pltpu.VMEM((16, 96, 128), BF16),
            pltpu.VMEM((16, 96, 128), BF16),
            pltpu.VMEM((128, 1536), BF16),
            pltpu.VMEM((128, 1536), BF16),
            pltpu.VMEM((160, 1536), BF16),
            pltpu.VMEM((160, 1536), BF16),
            pltpu.VMEM((128, 1536), BF16),
            pltpu.VMEM((128, 1536), BF16),
            pltpu.VMEM((256, 768), BF16),
            pltpu.VMEM((16, 96, 128), BF16),
            pltpu.VMEM((128, 1536), F32),
            pltpu.VMEM((1536, 896), BF16),
            dma((2,)), dma((2,)),
            dma((16,)), dma((16,)), dma((16,)), dma((16,)), dma((4,)), dma((4,)),
            dma((16,)), dma((16,)), dma((1,)), dma((1,)), dma((2,)), dma((2,)), dma((2,)),
            dma((2,)),
        ],
        compiler_params=pltpu.CompilerParams(
            collective_id=1, has_side_effects=True, vmem_limit_bytes=VMEM_BYTES
        ),
        name="middle",
    )(lengths, att, resid, cotangent, w_out, taps)


def backward_kernel(
    qt_ref, kvt_ref, dot_ref, mean_ref, probs_ref, weight_ref,
    gq_out, gk_out, gv_out, gw_out, taps_out,
    values, key_cols, dot_cols, dot_rows, query_rows_ref, weights, sum_k, sum_v, sum_q,
    part_mine, part_sent, part_got, back_kv, back_q, got_kv, got_q, final,
    shares, share_sum, share_send, share_got, total_ref, pair_got,
    probs_sems, ws_send, ws_recv, part_send, part_recv, kv_send, kv_recv, q_send, q_recv,
    group_send, group_recv, pair_send, pair_recv, out_send, out_recv, out_local,
):
    me = lax.axis_index("ctx")
    group = lax.axis_index("dp")
    core, chip = lax.rem(me, 2), me // 2
    sibling = me + 1 - 2 * core
    half, place = chip // 16, lax.rem(chip, 16)
    barrier_all(me, 64, 4)

    def send_share(step, carry):
        to = nth_chip(chip, core, step)
        rows = pl.ds(pl.multiple_of(to * 48, 48), 48)
        send_block(
            me, to * 2 + core, weight_ref.at[rows], shares.at[chip], ws_send.at[to], ws_recv.at[chip]
        )
        return carry

    lax.fori_loop(0, 32, send_share, 0)

    def fetch(chunk, slot):
        rows = pl.ds(pl.multiple_of(chunk * 512, 512), 512)
        return pltpu.make_async_copy(probs_ref.at[rows], weights.at[slot], probs_sems.at[slot])

    fetch(0, 0).start()

    def build_keys(tile, carry):
        one = lax.broadcasted_iota(jnp.int32, (32, TILE), 0) < 3
        ones = jnp.where(one, 1.0, 0.0).astype(BF16)
        wide = jnp.concatenate([kvt_ref[tile, 96:192, :], ones], axis=0)
        values[pl.ds(pl.multiple_of(tile * TILE, TILE), TILE), :] = wide.T
        lanes = pl.ds(pl.multiple_of(lax.rem(tile, 4) * TILE, TILE), TILE)
        key_cols[tile // 4, :, lanes] = kvt_ref[tile, 0:96, :]
        return carry

    lax.fori_loop(0, 32, build_keys, 0)

    def build_queries(tile, carry):
        mean = mean_ref[tile, 0:96, :]
        inverse = mean_ref[tile, 96:97, :]
        scaled = (dot_ref[tile].astype(F32) * inverse).astype(BF16)
        row_dot = jnp.sum(scaled.astype(F32) * mean, axis=0, keepdims=True)
        parts = three_parts(row_dot)
        row = lax.broadcasted_iota(jnp.int32, (32, TILE), 0)
        extra = jnp.zeros((32, TILE), F32)
        for n in range(3):
            extra = jnp.where(row == n, -parts[n], extra)
        wide = jnp.concatenate([scaled, extra.astype(BF16)], axis=0)
        rows = pl.ds(pl.multiple_of(tile * TILE, TILE), TILE)
        dot_cols[:, rows] = wide
        dot_rows[rows, :] = wide.T
        query = jnp.concatenate([qt_ref[tile], jnp.zeros((32, TILE), BF16)], axis=0)
        query_rows_ref[rows, :] = query.T
        return carry

    lax.fori_loop(0, 16, build_queries, 0)
    sum_q[...] = jnp.zeros_like(sum_q)

    def send_back(chunk):
        for n in range(2):
            index = 2 * chunk + n
            arrived(part_got.at[index], part_recv.at[index])
            total = part_mine[index] + part_got[index].astype(F32)
            back_kv[index] = total.astype(BF16)
            send_block(
                me, (2 * index + core) * 2 + half, back_kv.at[index], got_kv.at[place],
                kv_send.at[index], kv_recv.at[place],
            )

    def per_chunk(chunk, carry):
        slot = lax.rem(chunk, 2)
        fetch(chunk, slot).wait()

        @pl.when(chunk < 7)
        def _():
            fetch(chunk + 1, 1 - slot).start()

        rows = pl.ds(pl.multiple_of(chunk * 512, 512), 512)
        weight = weights[slot]
        dprob = jnp.dot(values[rows, :], dot_cols[...], preferred_element_type=F32)
        dscore = (weight.astype(F32) * dprob).astype(BF16)
        sum_v[...] = jnp.dot(weight, dot_rows[...], preferred_element_type=F32)
        sum_k[...] = jnp.dot(dscore, query_rows_ref[...], preferred_element_type=F32)
        sum_q[...] += jnp.dot(key_cols[chunk], dscore, preferred_element_type=F32)

        @pl.when(chunk > 0)
        def _():
            send_back(chunk - 1)

        for n in range(2):
            index = 2 * chunk + n
            for kind, sums, factor in ((0, sum_k, SCALE), (1, sum_v, 1.0)):
                first = pl.ds(pl.multiple_of((2 * n + core) * TILE, TILE), TILE)
                second = pl.ds(pl.multiple_of((2 * n + 1 - core) * TILE, TILE), TILE)
                features = slice(kind * 96, kind * 96 + 96)
                part_mine[index, features, :] = sums[first, :].T[0:96] * factor
                part_sent[index, features, :] = (sums[second, :].T[0:96] * factor).astype(BF16)
            remote(
                part_sent.at[index], part_got.at[index], part_send.at[index], part_recv.at[index],
                ctx=sibling,
            ).start()
        return carry

    lax.fori_loop(0, 8, per_chunk, 0)

    for n in range(16):
        back_q[n] = (sum_q[:, n * TILE : (n + 1) * TILE] * SCALE).astype(BF16)
    send_heads(me, back_q, got_q, place, half, q_send, q_recv.at[place])
    send_back(7)

    share_sum[...] = jnp.zeros_like(share_sum)

    def add_share(step, carry):
        slot = nth_chip(chip, core, step)
        arrived(shares.at[slot], ws_recv.at[slot])
        share_sum[...] += shares[slot].astype(F32)
        return carry

    lax.fori_loop(0, 32, add_share, 0)
    share_send[...] = share_sum[...].astype(BF16)
    for step in range(1, 4):
        remote(
            share_send, share_got.at[step - 1], group_send.at[step - 1], group_recv.at[step - 1],
            dp=lax.rem(group + step, 4),
        ).start()

    def tile_back(n, t):
        pieces = []
        for u in range(4):
            feature = t * TILE + u * 32
            head, first = feature // 96, feature % 96
            if n == 0:
                pieces.append(got_q[head, first : first + 32, :])
            else:
                first = first + (n - 1) * 96
                pieces.append(got_kv[head, first : first + 32, :])
        final[n, :, t * TILE : (t + 1) * TILE] = jnp.concatenate(pieces, axis=0).T

    mine = pl.ds(pl.multiple_of(core * 64, 64), 64)
    other = pl.ds(pl.multiple_of((1 - core) * 64, 64), 64)
    outs = (gq_out, gk_out, gv_out)

    def out_copies(n):
        there = remote(
            final.at[n, other], outs[n].at[core], out_send.at[n], out_recv.at[n], ctx=sibling
        )
        here = pltpu.make_async_copy(final.at[n, mine], outs[n].at[core], out_local.at[n])
        return there, here

    def kv_arrived(step, carry):
        arrived(got_kv.at[step], kv_recv.at[step])
        return carry

    def q_arrived(step, carry):
        arrived(got_q.at[step], q_recv.at[step])
        return carry

    lax.fori_loop(0, 16, q_arrived, 0)
    for n in (0, 1, 2):
        if n == 1:
            lax.fori_loop(0, 16, kv_arrived, 0)
        for t in range(12):
            tile_back(n, t)
        there, here = out_copies(n)
        there.start()
        here.start()

    for step in range(3):
        arrived(share_got.at[step], group_recv.at[step])
        share_sum[...] += share_got[step].astype(F32)
    total_ref[...] = share_sum[...] * (1.0 / math.sqrt(32768))
    give = pl.ds(pl.multiple_of((1 - core) * 24, 8), 24)
    keep = pl.ds(pl.multiple_of(core * 24, 8), 24)
    pair = remote(total_ref.at[give], pair_got, pair_send.at[0], pair_recv.at[0], ctx=sibling)
    pair.start()
    pair.wait_recv()
    own_half = pl.ds(pl.multiple_of(core * 768, 768), 768)
    other_half = pl.ds(pl.multiple_of((1 - core) * 768, 768), 768)
    gw_out[:, own_half] = total_ref[keep, 0:768]
    gw_out[:, other_half] = pair_got[:, 0:768]
    taps_out[...] = total_ref[keep, 768:896] + pair_got[:, 768:896]

    pair.wait_send()
    for step in range(3):
        arrived(share_send, group_send.at[step])

    def all_sent(step, carry):
        @pl.when(step * 2 + core != me)
        def _():
            arrived(weight_ref.at[pl.ds(0, 48)], ws_send.at[step])

        return carry

    lax.fori_loop(0, 32, all_sent, 0)

    def parts_sent(step, carry):
        arrived(part_sent.at[step], part_send.at[step])

        @pl.when((2 * step + core) * 2 + half != me)
        def _():
            arrived(back_kv.at[step], kv_send.at[step])

        return carry

    lax.fori_loop(0, 16, parts_sent, 0)
    heads_sent(me, back_q, half, q_send)
    for n in range(3):
        there, here = out_copies(n)
        here.wait()
        there.wait_send()
        there.wait_recv()


def attend_backward(qt, kvt, dot, mean, probs, weight):
    dma = pltpu.SemaphoreType.DMA
    grads = jax.ShapeDtypeStruct((2, 64, 1536), BF16)
    return pl.pallas_call(
        backward_kernel,
        out_shape=(
            grads,
            grads,
            grads,
            jax.ShapeDtypeStruct((24, 1536), F32),
            jax.ShapeDtypeStruct((24, 128), F32),
        ),
        in_specs=[IN_VMEM] * 4 + [ANY] * 2,
        out_specs=[ANY] * 3 + [IN_VMEM] * 2,
        scratch_shapes=[
            pltpu.VMEM((4096, 128), BF16),
            pltpu.VMEM((8, 96, 512), BF16),
            pltpu.VMEM((128, 2048), BF16),
            pltpu.VMEM((2048, 128), BF16),
            pltpu.VMEM((2048, 128), BF16),
            pltpu.VMEM((2, 512, 2048), BF16),
            pltpu.VMEM((512, 128), F32),
            pltpu.VMEM((512, 128), F32),
            pltpu.VMEM((96, 2048), F32),
            pltpu.VMEM((16, 192, 128), F32),
            pltpu.VMEM((16, 192, 128), BF16),
            pltpu.VMEM((16, 192, 128), BF16),
            pltpu.VMEM((16, 192, 128), BF16),
            pltpu.VMEM((16, 96, 128), BF16),
            pltpu.VMEM((16, 192, 128), BF16),
            pltpu.VMEM((16, 96, 128), BF16),
            pltpu.VMEM((3, 128, 1536), BF16),
            pltpu.VMEM((32, 48, 896), BF16),
            pltpu.VMEM((48, 896), F32),
            pltpu.VMEM((48, 896), BF16),
            pltpu.VMEM((3, 48, 896), BF16),
            pltpu.VMEM((48, 896), F32),
            pltpu.VMEM((24, 896), F32),
            dma((2,)), dma((32,)), dma((32,)), dma((16,)), dma((16,)), dma((16,)), dma((16,)),
            dma((16,)), dma((16,)), dma((3,)), dma((3,)), dma((1,)), dma((1,)), dma((3,)),
            dma((3,)), dma((3,)),
        ],
        compiler_params=pltpu.CompilerParams(
            collective_id=2, has_side_effects=True, vmem_limit_bytes=VMEM_BYTES
        ),
        name="attend_backward",
    )(qt, kvt, dot, mean, probs, weight)


def deliver_kernel(a_in, b_in, c_in, d_in, e_in, w_in, taps_in, a, b, c, d, e, w, taps):
    for source, target in ((a_in, a), (b_in, b), (c_in, c), (d_in, d), (e_in, e)):
        target[...] = source[...]
    w[...] = w_in[...]
    taps[...] = taps_in[...].T[0:31, :]


def deliver(rows, grad_w, grad_taps):
    frames = pl.BlockSpec((1, 64, 1536), lambda n: (n, 0, 0))
    weights = pl.BlockSpec((24, 1536), lambda n: (0, 0))
    shape = jax.ShapeDtypeStruct((2, 64, 1536), BF16)
    return pl.pallas_call(
        deliver_kernel,
        grid=(2,),
        out_shape=(shape,) * 5
        + (jax.ShapeDtypeStruct((24, 1536), F32), jax.ShapeDtypeStruct((31, 24), F32)),
        in_specs=[frames] * 5 + [weights, pl.BlockSpec((24, 128), lambda n: (0, 0))],
        out_specs=[frames] * 5 + [weights, pl.BlockSpec((31, 24), lambda n: (0, 0))],
        name="deliver",
    )(*rows, grad_w, grad_taps)


def per_device(resid, queries, keys_in, values, w_out, slopes, kernel, lengths, cotangent):
    qt, kvt = spread_heads(queries, keys_in, values)
    att, mean, probs = attend_forward(slopes, lengths, qt, kvt)
    block_out, grad_resid, dot, weight = middle(lengths, att, resid, cotangent, w_out, kernel)
    grad_q, grad_k, grad_v, grad_w, grad_taps = attend_backward(qt, kvt, dot, mean, probs, weight)
    return deliver((block_out, grad_resid, grad_q, grad_k, grad_v), grad_w, grad_taps)


def solution(mesh):
    spread = P("dp", "ctx", None)
    in_specs = (spread, spread, spread, spread, P(), P(), P(), P("dp"), spread)
    out_specs = (spread, spread, spread, spread, spread, P("ctx", None), P(None, "ctx"))
    return jax.shard_map(
        per_device, mesh=mesh, in_specs=in_specs, out_specs=out_specs, check_vma=False
    )
```
